512 devices in a mesh: dp: 64 (over x, z), tensor: 8 (over y, core).
Axes of the slice: x: 4, y: 4, z: 16, core: 2. Of those that a mesh axis runs over, the one named last changes fastest.
Arguments:
- ctx: bfloat16 [16384, 5120], P('dp', 'tensor'), may hold values from -16 to 16
- resid: bfloat16 [16384, 5120], P('dp', 'tensor'), may hold values from -6 to 6
- output_projection_weight: bfloat16 [5120, 5120], P('tensor', 'dp'), may hold values from -0.078125 to 0.078125
- adapter_down_weight: bfloat16 [5120, 64], P('tensor'), may hold values from -0.078125 to 0.078125
- adapter_up_weight: bfloat16 [64, 5120], P(None, 'tensor'), may hold values from -0.75 to 0.75
- down_direction: bfloat16 [5120, 64], P('tensor'), may hold values from -0.078125 to 0.078125
- up_direction: bfloat16 [64, 5120], P(None, 'tensor'), may hold values from -0.75 to 0.75
- layer_norm_gain: float32 [5120], P('tensor'), may hold values from 0.25 to 1.75
- lengths: int32 [128], P('dp'), may hold values from 1 to 128, as said below
Outputs:
- hvp_a: float32 [5120, 64], P(('tensor', 'dp'))
- hvp_b: float32 [64, 5120], P('dp', 'tensor')
The draws below stay inside these ranges and needn't reach their ends.
Inputs may be any that keep to these rules, and one draw needn't show every extreme that they name: `lengths`: some sequence is full in every draw.
All inputs are finite; a program needn't handle non-finite values.
Results may differ from the reference program's by a relative error of at most 0.0008.
Values may be sent and summed in bfloat16 or wider, within the bound.
A program may use at most 64 MiB of HBM per device.

```python
import jax
import jax.numpy as jnp
from jax import lax

MODEL_WIDTH = 5120
ADAPTER_RANK = 64
SEQ_LEN = 128
TOKENS = 16384
SEQS = 128
N_TENSOR = 8


def draw_lengths(key, part):
    key = jax.random.fold_in(key, 7)
    first, second = jax.random.split(key)
    values = jax.random.randint(first, (SEQS,), 1, SEQ_LEN + 1)
    spot = jax.random.randint(second, (), 0, SEQS)
    return jnp.where(jnp.arange(SEQS) == spot, SEQ_LEN, values).astype(jnp.int32)


def raised(array, stream_key, source, target, blocks, factor):
    def block_of(dim):
        return (jnp.arange(array.shape[dim]) // (array.shape[dim] // blocks)).reshape((-1,) + (1,) * (array.ndim - 1 - dim))

    one_side = jax.random.permutation(stream_key, blocks)[block_of(target)]
    far = (block_of(target) + blocks // 2) % blocks
    return jnp.where((block_of(source) == one_side) | (block_of(source) == far), factor * array, array)


def block_levels(key, dims, cuts, smallest, high):
    factor_of = 1.0
    for axis_at, parts in cuts:
        heights = jax.random.uniform(jax.random.fold_in(jax.random.fold_in(key, 6), axis_at), (parts,), jnp.float32, smallest / len(cuts), high / len(cuts))
        factor_of = factor_of * jnp.repeat(jnp.exp(heights), dims[axis_at] // parts).reshape((-1,) + (1,) * (len(dims) - 1 - axis_at))
    return factor_of


def scatter_about(rng, shape, deviation, bound, shards=(), held_as=jnp.bfloat16):
    level = block_levels(rng, shape, shards, -0.22, 0.18) if shards else 1.0
    array = jax.random.normal(rng, shape, jnp.float32) * deviation * level
    return jnp.minimum(jnp.maximum(array, -bound), bound).astype(held_as)


def noise_with(key, extent, deviation, reach, shards, heavy, held_as=jnp.bfloat16):
    values = deviation * jax.random.normal(key, extent, jnp.float32)
    if shards:
        values = values * block_levels(key, extent, shards, -0.22, 0.18)
    return jnp.clip(raised(values, jax.random.fold_in(key, 3), *heavy), -reach, reach).astype(held_as)


def setup_inputs(seed: int = 0) -> dict:
    key_of = jax.random.split(jax.random.key(seed), 10)
    return {
        "ctx": noise_with(key_of[0], (TOKENS, MODEL_WIDTH), 1.0, 16.0, ((0, 64), (1, 8)), (0, 1, 64, 4.0)),
        "resid": scatter_about(key_of[1], (TOKENS, MODEL_WIDTH), 1.0, 6.0, ((0, 64), (1, 8))),
        "output_projection_weight": scatter_about(key_of[2], (MODEL_WIDTH, MODEL_WIDTH), MODEL_WIDTH ** -0.5, 0.078125, ((0, 8), (1, 64))),
        "adapter_down_weight": scatter_about(key_of[3], (MODEL_WIDTH, ADAPTER_RANK), MODEL_WIDTH ** -0.5, 0.078125, ((0, 8),)),
        "adapter_up_weight": scatter_about(key_of[4], (ADAPTER_RANK, MODEL_WIDTH), ADAPTER_RANK ** -0.5, 0.75, ((1, 8),)),
        "down_direction": scatter_about(key_of[5], (MODEL_WIDTH, ADAPTER_RANK), MODEL_WIDTH ** -0.5, 0.078125, ((0, 8),)),
        "up_direction": scatter_about(key_of[6], (ADAPTER_RANK, MODEL_WIDTH), ADAPTER_RANK ** -0.5, 0.75, ((1, 8),)),
        "layer_norm_gain": jnp.clip(1.0 + 0.15 * jax.random.normal(key_of[7], (MODEL_WIDTH,), jnp.float32), 0.25, 1.75),
        "lengths": draw_lengths(jax.random.fold_in(key_of[9], 71), 0),
    }


def reference(ctx, resid, output_projection_weight, adapter_down_weight, adapter_up_weight, down_direction, up_direction, layer_norm_gain, lengths):
    block = MODEL_WIDTH // N_TENSOR
    attn = jnp.zeros((TOKENS, MODEL_WIDTH), jnp.float32)
    for index in range(N_TENSOR):
        piece = jnp.dot(ctx[:, index * block:(index + 1) * block], output_projection_weight[index * block:(index + 1) * block, :], preferred_element_type=jnp.float32)
        rounded = lax.optimization_barrier(piece.astype(jnp.bfloat16))
        attn = attn + rounded.astype(jnp.float32)
    high = lax.Precision.HIGHEST
    reduced_rank_output = jnp.dot(ctx, adapter_down_weight, preferred_element_type=jnp.float32)
    low_tangent = jnp.dot(ctx, down_direction, preferred_element_type=jnp.float32)
    raised_output = adapter_up_weight.astype(jnp.float32)
    up_tangent = up_direction.astype(jnp.float32)
    hidden = attn + jnp.dot(reduced_rank_output, raised_output, precision=high) + resid.astype(jnp.float32)
    center = lax.optimization_barrier(jnp.mean(hidden, axis=1, keepdims=True))
    spread = lax.optimization_barrier(jnp.mean(hidden * hidden, axis=1, keepdims=True)) - center * center
    inverse = lax.rsqrt(spread + 1e-05)
    normed = (hidden - center) * inverse
    tangent = jnp.dot(low_tangent, raised_output, precision=high) + jnp.dot(reduced_rank_output, up_tangent, precision=high)
    tangent_n = inverse * (tangent - lax.optimization_barrier(jnp.mean(tangent, axis=1, keepdims=True)) - normed * lax.optimization_barrier(jnp.mean(normed * tangent, axis=1, keepdims=True)))
    position = jnp.arange(TOKENS, dtype=jnp.int32)
    limit = jnp.repeat(lengths, SEQ_LEN)
    live = (position % SEQ_LEN < limit).astype(jnp.float32) / jnp.sqrt(jnp.float32(TOKENS))
    cotangent = live[:, None] * (layer_norm_gain * layer_norm_gain)[None, :] * tangent_n
    grad_h = inverse * (cotangent - lax.optimization_barrier(jnp.mean(cotangent, axis=1, keepdims=True)) - normed * lax.optimization_barrier(jnp.mean(normed * cotangent, axis=1, keepdims=True)))
    hvp_b = jnp.dot(reduced_rank_output.T, grad_h, precision=high)
    projected = jnp.dot(grad_h, raised_output.T, precision=high)
    hvp_a = jnp.dot(ctx.astype(jnp.float32).T, projected, precision=high)
    return (hvp_a, hvp_b)
```

```python
import functools

import jax
import jax.numpy as jnp
from jax import lax
from jax.experimental import pallas as pl
from jax.experimental.pallas import tpu as pltpu
from jax.sharding import Mesh, PartitionSpec as P

AXES = ("x", "z", "y", "c")
NX, NZ, NY, NC = 4, 16, 4, 2
SEQ = 128
RANK = 64
FEATS = 1280
HALF = 640
COLS = 80
TOKENS = 16384
WIDTH = 5120
BF = jnp.bfloat16
F32 = jnp.float32
CHUNKS = ((0, 7), (7, 9), (9, 11), (11, 13), (13, 15), (15, 16))
NCH = len(CHUNKS)
NT = (((1,), (1,)), ((), ()))
TN = (((0,), (0,)), ((), ()))


def split2(v):
    hi = v.astype(BF)
    lo = (v - hi.astype(F32)).astype(BF)
    return hi, lo


def split3(v):
    hi = v.astype(BF)
    rest = v - hi.astype(F32)
    mid = rest.astype(BF)
    lo = (rest - mid.astype(F32)).astype(BF)
    return hi, mid, lo


def dot(a, b, dims=(((1,), (0,)), ((), ()))):
    return lax.dot_general(a, b, dims, preferred_element_type=F32)


def kernel(
    ctx_ref, resid_ref, wt_ref, at_ref, dt_ref, b_ref, u_ref, g_ref, len_ref,
    out_a, out_b,
    ctxg, wg, adg, rt, rrecv, buT, gr, part, rsb, zpart, zb, h_ref, dh_ref, gh_ref,
    st_snd, st_rcv, qg, ha_snd, ha_rcv, hb_snd, hb_rcv, ha_sum, hb_sum, buf2, rcv2,
    s_ctx, r_ctx, s_w, r_w, s_ws, r_ws, s_ad, r_ad, s_res, r_res, s_bu, r_bu, s_rs, r_rs,
    s_z, r_z, s_st, r_st, s_q, r_q, s_ha, r_ha, s_hb, r_hb, s_2, r_2,
):
    x, z, y, c = [lax.axis_index(a) for a in AXES]

    def dev(dx=0, dz=0, dy=0, dc=0):
        return (lax.rem(x + dx + NX, NX), lax.rem(z + dz + NZ, NZ), lax.rem(y + dy + NY, NY), lax.rem(c + dc, NC))

    def rcopy(src, dst, ss, rs, to):
        return pltpu.make_async_remote_copy(
            src_ref=src, dst_ref=dst, send_sem=ss, recv_sem=rs, device_id=to, device_id_type=pl.DeviceIdType.MESH
        )

    barrier = pltpu.get_barrier_semaphore()
    count = 0
    for dx in range(NX):
        for dy in range(NY):
            for dc in range(NC):
                if (dx, dy, dc) != (0, 0, 0):
                    pl.semaphore_signal(barrier, inc=1, device_id=dev(dx, 0, dy, dc), device_id_type=pl.DeviceIdType.MESH)
                    count += 1
    for dz in range(1, NZ):
        pl.semaphore_signal(barrier, inc=1, device_id=dev(0, dz), device_id_type=pl.DeviceIdType.MESH)
        count += 1
    pl.semaphore_wait(barrier, count)

    pending = []
    diag = x == y

    wr = {}

    def w_start(s, flow, src, lanes=None):
        slot = 15 if s == 8 else (2 * s - 1 if flow == 0 else 2 * s)
        dst = wg.at[c, slot]
        if s == 8:
            lanes = pl.ds(0, 384) if flow == 0 else pl.ds(384, 256)
            src, dst = src.at[:, lanes], dst.at[:, lanes]
        k = 2 * (s - 1) + flow
        cp = rcopy(src, dst, s_w.at[k], r_w.at[k], dev(0, 1 if flow == 0 else -1))
        cp.start()
        wr[(s, flow)] = cp
        pending.append(cp)

    def w_sib(slot, src):
        cp = rcopy(src, wg.at[c, slot], s_ws.at[slot], r_ws.at[slot], dev(0, 0, 0, 1))
        cp.start()
        pending.append(cp)
        return cp

    w_start(1, 0, wt_ref)
    w_start(1, 1, wt_ref)
    ctx_cp = {}
    for half in range(2):
        src = ctx_ref.at[pl.ds(half * SEQ, SEQ), :]
        for k, dx in ((1, 1), (3, -1)):
            i = (0 if dx == 1 else 2) + half
            to = (lax.rem(x + dx + NX, NX), z, y, half)
            cp = rcopy(src, ctxg.at[x, c], s_ctx.at[i], r_ctx.at[k + c], to)
            cp.start()
            pending.append(cp)
    sib_half = lax.rem(c + 1, 2)
    cp = rcopy(ctx_ref.at[pl.ds(pl.multiple_of(sib_half * SEQ, SEQ), SEQ), :], ctxg.at[x, c], s_ctx.at[4], r_ctx.at[0], dev(0, 0, 0, 1))
    cp.start()
    pending.append(cp)
    sib = [w_sib(0, wt_ref)]
    adg[c, 0:RANK] = at_ref[...]
    adg[c, RANK:] = dt_ref[...]
    ad_cp = rcopy(adg.at[c], adg.at[c], s_ad.at[0], r_ad.at[0], dev(0, 0, 0, 1))
    ad_cp.start()
    pending.append(ad_cp)
    wg[c, 0] = wt_ref[...]
    ctxg[x, c] = ctx_ref[pl.ds(pl.multiple_of(c * SEQ, SEQ), SEQ), :]

    lane = lax.broadcasted_iota(jnp.int32, (16, SEQ), 1)
    to_y = lax.rem(2 * y - x + 2 * NY, NY)
    for half in range(2):
        rt[half, 0:HALF] = resid_ref[half * SEQ:(half + 1) * SEQ, :].T
        rt[half, HALF:] = jnp.where(lane < len_ref[half], 1.0, 0.0).astype(BF)
        mine = jnp.logical_and(diag, c == half)

        @pl.when(jnp.logical_not(mine))
        def _():
            rcopy(rt.at[half], rrecv.at[c], s_res.at[half], r_res.at[c], (y, z, to_y, half)).start()

        @pl.when(mine)
        def _():
            rrecv[c] = rt[half]

    @pl.when(diag)
    def _():
        buT[c] = jnp.concatenate([b_ref[...], u_ref[...]], axis=0).T
        gr[c, 0:5] = g_ref[...]
        gr[c, 5:8] = jnp.zeros((3, SEQ), F32)
        for dy in range(1, NY):
            rcopy(buT.at[c], buT.at[c], s_bu.at[dy - 1], r_bu.at[0], dev(0, 0, dy)).start()
            rcopy(gr.at[c], gr.at[c], s_bu.at[dy + 2], r_bu.at[1], dev(0, 0, dy)).start()

    @pl.when(jnp.logical_not(diag))
    def _():
        rcopy(buT.at[c], buT.at[c], s_bu.at[0], r_bu.at[0], dev(0, 0, 1)).wait_recv()
        rcopy(gr.at[c], gr.at[c], s_bu.at[3], r_bu.at[1], dev(0, 0, 1)).wait_recv()

    bu_s = rcopy(buT.at[c], buT.at[c], s_bu.at[6], r_bu.at[2], dev(0, 0, 0, 1))
    gr_s = rcopy(gr.at[c], gr.at[c], s_bu.at[7], r_bu.at[3], dev(0, 0, 0, 1))
    bu_s.start()
    gr_s.start()
    pending.extend([bu_s, gr_s])

    def block(j):
        return lax.rem(x + j, NX)

    def z_item(j):
        xb = block(j)
        zpart[j] = dot(adg[0], ctxg[xb, 0], NT) + dot(adg[1], ctxg[xb, 1], NT)
        dest = lax.rem(x - j + NY, NY)
        dy = lax.rem(dest - y + NY, NY)

        @pl.when(dest != y)
        def _():
            rcopy(zpart.at[j], zb.at[y], s_z.at[j], r_z.at[dy], (x, z, dest, c)).start()

    def mm_item(j, k):
        lo, hi = CHUNKS[k]
        rows = (hi - lo) * COLS
        xb = block(j)
        w0 = wg[0, lo:hi].reshape(rows, HALF)
        w1 = wg[1, lo:hi].reshape(rows, HALF)
        part[j, lo * COLS:hi * COLS] = (dot(w0, ctxg[xb, 0], NT) + dot(w1, ctxg[xb, 1], NT)).astype(BF)
        dest = lax.rem(x - j + NY, NY)
        dy = lax.rem(dest - y + NY, NY)
        piece = pl.ds(lo * COLS, rows)

        @pl.when(dest != y)
        def _():
            rcopy(part.at[j, piece], rsb.at[y, piece], s_rs.at[j, k], r_rs.at[dy, k], (x, z, dest, c)).start()

    def w_wait(s):
        for flow in range(2):
            wr[(s, flow)].wait_recv()
            if s < 8:
                slot = 2 * s - 1 if flow == 0 else 2 * s
                if s < 7 or True:
                    w_start(s + 1, flow, wg.at[c, slot])
                sib.append(w_sib(slot, wg.at[c, slot]))
        if s == 8:
            sib.append(w_sib(15, wg.at[c, 15]))

    def sib_wait(slots):
        for slot in slots:
            rcopy(wg.at[c, slot], wg.at[c, slot], s_ws.at[slot], r_ws.at[slot], dev(0, 0, 0, 1)).wait_recv()

    def ctx_wait(i):
        rcopy(ctxg.at[0, 0], ctxg.at[0, 0], s_ctx.at[4], r_ctx.at[i], dev(0, 0, 0, 1)).wait_recv()

    def ctx_forward(i, dx_src, half_c, to_dx, sem):
        xb = lax.rem(x + dx_src + NX, NX)
        cp = rcopy(ctxg.at[xb, half_c], ctxg.at[xb, half_c], s_ctx.at[sem], r_ctx.at[i], dev(to_dx))
        cp.start()
        pending.append(cp)

    ctx_wait(0)
    ad_cp.wait_recv()
    z_item(0)
    w_wait(1)
    w_wait(2)
    for i in (1, 2, 3, 4):
        ctx_wait(i)
        if i == 1:
            ctx_forward(5, -1, 0, 1, 5)
        if i == 4:
            ctx_forward(6, 1, 1, -1, 6)
    z_item(1)
    z_item(3)
    w_wait(3)
    sib_wait(range(0, 7))
    for j in (0, 1, 3):
        mm_item(j, 0)
    w_wait(4)
    sib_wait((7, 8))
    for j in (0, 1, 3):
        mm_item(j, 1)
    ctx_wait(5)
    ctx_wait(6)
    w_wait(5)
    z_item(2)
    mm_item(2, 0)
    mm_item(2, 1)
    for s in range(5, 9):
        if s > 5:
            w_wait(s)
        sib_wait((9, 10) if s == 5 else ((15,) if s == 8 else (2 * s - 1, 2 * s)))
        for j in (2, 1, 3, 0):
            mm_item(j, s - 3)

    bu_s.wait_recv()
    gr_s.wait_recv()
    for cc in range(2):
        @pl.when(jnp.logical_not(jnp.logical_and(diag, c == cc)))
        def _():
            rcopy(rrecv.at[cc], rrecv.at[cc], s_res.at[cc], r_res.at[cc], dev(0, 0, 0, 1)).wait_recv()
    jown = lax.rem(x - y + NX, NX)
    zz = zpart[jown]
    for dy in range(1, NY):
        ys = lax.rem(y - dy + NY, NY)
        rcopy(zb.at[ys], zb.at[ys], s_z.at[0], r_z.at[dy], dev(0, 0, dy)).wait_recv()
        zz = zz + zb[ys]
    zt = zz[0:RANK]
    ztt = zz[RANK:]
    zero = jnp.zeros((RANK, SEQ), F32)
    rhs = jnp.concatenate([jnp.concatenate([ztt, zt], axis=0), jnp.concatenate([zt, zero], axis=0)], axis=1)
    r1, r2, r3 = split3(rhs)
    for cc in range(2):
        m = buT[cc]
        both = dot(m, r1) + dot(m, r2) + dot(m, r3)
        dh_ref[cc * HALF:(cc + 1) * HALF] = both[:, 0:SEQ]
        h_ref[cc * HALF:(cc + 1) * HALF] = both[:, SEQ:] + rrecv[cc, 0:HALF].astype(F32)
    live = rrecv[0, HALF:].astype(F32)[0:1] * (1.0 / jnp.sqrt(jnp.float32(TOKENS)))

    for k, (lo, hi) in enumerate(CHUNKS):
        for dy in range(1, NY):
            ys = lax.rem(y - dy + NY, NY)
            piece = pl.ds(lo * COLS, (hi - lo) * COLS)
            rcopy(rsb.at[ys, piece], rsb.at[ys, piece], s_rs.at[0, k], r_rs.at[dy, k], dev(0, 0, dy)).wait_recv()
        for slot in range(lo, hi):
            step = (slot + 1) // 2
            zz_ = z if slot == 0 else (z - step if slot % 2 == 1 else z + step)
            zz_ = lax.rem(zz_ + NZ, NZ)
            rows = pl.ds(pl.multiple_of(zz_ * COLS, 16), COLS)
            piece = pl.ds(slot * COLS, COLS)
            acc = part[jown, piece].astype(F32)
            for dy in range(1, NY):
                ys = lax.rem(y - dy + NY, NY)
                acc = acc + rsb[ys, piece].astype(F32)
            h_ref[rows] = h_ref[rows] + acc

    def gsq(i):
        row = gr[i // 5, pl.ds(i % 5, 1)]
        col = jnp.broadcast_to(row, (SEQ, SEQ)).T
        return col * col

    sums = [jnp.zeros((8, SEQ), F32) for _ in range(9)]

    def fold(v):
        return jnp.sum(v.reshape(16, 8, SEQ), axis=0)

    for i in range(10):
        rows = pl.ds(i * SEQ, SEQ)
        h = h_ref[rows]
        d = dh_ref[rows]
        g2 = gsq(i)
        gh_ref[rows] = g2
        hd = h * d
        hh = h * h
        terms = (h, hh, d, hd, g2 * d, g2, g2 * h, g2 * hh, g2 * hd)
        sums = [s + fold(t) for s, t in zip(sums, terms)]
    for n, s in enumerate(sums):
        st_snd[n:n + 1] = jnp.sum(s, axis=0, keepdims=True)
    st_snd[9:] = jnp.zeros((7, SEQ), F32)
    st_cp = []
    for dx in range(1, NX):
        to = (lax.rem(x + dx, NX), z, lax.rem(y + 2 * dx, NY), c)
        cp = rcopy(st_snd, st_rcv.at[dx], s_st.at[dx], r_st.at[dx], to)
        cp.start()
        st_cp.append(cp)
    total = st_snd[...]
    for cp, dx in zip(st_cp, range(1, NX)):
        cp.wait()
        total = total + st_rcv[dx]
    total = total * (1.0 / WIDTH)
    e_h, e_hh, m1, e_hd, e_gd, e_g, e_gh, e_ghh, e_ghd = [total[n:n + 1] for n in range(9)]
    mu = e_h
    rinv = lax.rsqrt(e_hh - mu * mu + 1e-05)
    m2 = rinv * (e_hd - mu * m1)
    g_n = rinv * (e_gh - mu * e_g)
    g_nn = rinv * rinv * (e_ghh - 2.0 * mu * e_gh + mu * mu * e_g)
    g_nd = rinv * (e_ghd - mu * e_gd)
    lr = live * rinv
    m3 = lr * (e_gd - m1 * e_g - m2 * g_n)
    m4 = lr * (g_nd - m1 * g_n - m2 * g_nn)

    q = jnp.zeros((SEQ, 2 * SEQ), F32)
    z1, z2 = split2(zt)
    zs = jnp.concatenate([z1, z2], axis=0)
    for cc in range(2):
        rows = pl.ds(cc * HALF, HALF)
        n = (h_ref[rows] - mu) * rinv
        cot = lr * gh_ref[rows] * (dh_ref[rows] - m1 - n * m2)
        gh = rinv * (cot - m3 - n * m4)
        g1, g2 = split2(gh)
        q = q + dot(buT[cc], jnp.concatenate([g1, g2], axis=1), TN)
        hb = dot(zs, g1, NT) + dot(zs, g2, NT)
        hb = hb[0:RANK] + hb[RANK:]
        for p in range(NX):
            hb_snd[p, cc] = hb[16 * p:16 * (p + 1)]
    mine_b = 2 * x - y
    xq = lax.rem(mine_b + NX, NX)
    qg[xq] = q[0:RANK, 0:SEQ] + q[0:RANK, SEQ:]
    q_cp = []
    for dy in range(1, NY):
        cp = rcopy(qg.at[xq], qg.at[xq], s_q.at[dy], r_q.at[dy], dev(0, 0, dy))
        cp.start()
        q_cp.append(cp)

    for dp in range(NX):
        for dc in range(NC):
            p, cd = lax.rem(x + dp, NX), lax.rem(c + dc, NC)
            me = jnp.logical_and(diag, dp == 0 and dc == 0)

            @pl.when(jnp.logical_not(me))
            def _():
                rcopy(hb_snd.at[p, cd], hb_rcv.at[2 * y + c], s_hb.at[2 * dp + dc], r_hb.at[2 * y + c], (p, z, x, cd)).start()

    @pl.when(diag)
    def _():
        hb_rcv[2 * y + c] = hb_snd[x, c]

    for cp in q_cp:
        cp.wait()
    ha = [jnp.zeros((2 * RANK, HALF), F32) for _ in range(2)]
    for xb in range(NX):
        q1, q2 = split2(qg[xb])
        qs = jnp.concatenate([q1, q2], axis=0)
        ha = [ha[cc] + dot(qs, ctxg[xb, cc]) for cc in range(2)]
    low = lax.broadcasted_iota(jnp.int32, (COLS, SEQ), 1) < RANK
    for cc in range(2):
        t = ha[cc].T
        t = t + pltpu.roll(t, RANK, 1)
        for p in range(NX):
            ha_snd[p, cc] = jnp.where(low, t[160 * p:160 * p + COLS], t[160 * p + COLS:160 * (p + 1)])
    ha_cp = []
    for dx in range(NX):
        for dc in range(NC):
            if (dx, dc) != (0, 0):
                p, cd = lax.rem(x + dx, NX), lax.rem(c + dc, NC)
                i = 2 * dx + dc
                cp = rcopy(ha_snd.at[p, cd], ha_rcv.at[i], s_ha.at[i], r_ha.at[i], (p, z, y, cd))
                cp.start()
                ha_cp.append((i, cp))
    for i in range(8):
        me = jnp.logical_and(diag, 2 * y + c == i)

        @pl.when(jnp.logical_not(me))
        def _():
            rcopy(hb_rcv.at[i], hb_rcv.at[i], s_hb.at[i], r_hb.at[i], dev(0, 0, 0, 1)).wait_recv()
    acc = hb_rcv[0]
    for i in range(1, 8):
        acc = acc + hb_rcv[i]
    hb_sum[...] = acc
    acc = ha_snd[x, c]
    for i, cp in ha_cp:
        cp.wait()
        acc = acc + ha_rcv[i]
    ha_sum[...] = acc
    lowk = lax.broadcasted_iota(jnp.int32, (16, SEQ), 1) < RANK
    for k in range(10):
        a = ha_sum[pl.ds(k, 8, stride=10)]
        a = jnp.concatenate([a, pltpu.roll(a, RANK, 1)], axis=0)
        tile = hb_sum[:, (k // 2) * SEQ:(k // 2 + 1) * SEQ]
        if k % 2 == 0:
            tile = pltpu.roll(tile, RANK, 1)
        v = jnp.where(lowk, a, tile)
        for zi in range(NZ):
            buf2[zi, k:k + 1] = v[zi:zi + 1]
    cps = []
    for dz in range(1, NZ):
        zd = lax.rem(z + dz, NZ)
        cp = rcopy(buf2.at[zd], rcv2.at[dz], s_2.at[dz], r_2.at[dz], dev(0, dz))
        cp.start()
        cps.append(cp)
    acc = buf2[z]
    for dz, cp in zip(range(1, NZ), cps):
        cp.wait()
        acc = acc + rcv2[dz]
    out_a[...] = acc[0:10, 0:RANK]
    for k in range(10):
        out_b[0:1, k * RANK:(k + 1) * RANK] = acc[k:k + 1, RANK:]

    for cp in pending:
        cp.wait_send()
    for half in range(2):
        @pl.when(jnp.logical_not(jnp.logical_and(diag, c == half)))
        def _():
            rcopy(rt.at[half], rrecv.at[c], s_res.at[half], r_res.at[c], (y, z, to_y, half)).wait_send()

    @pl.when(diag)
    def _():
        for dy in range(1, NY):
            rcopy(buT.at[c], buT.at[c], s_bu.at[dy - 1], r_bu.at[0], dev(0, 0, dy)).wait_send()
            rcopy(gr.at[c], gr.at[c], s_bu.at[dy + 2], r_bu.at[1], dev(0, 0, dy)).wait_send()

    for j in range(NX):
        dest = lax.rem(x - j + NY, NY)

        @pl.when(dest != y)
        def _():
            rcopy(zpart.at[j], zb.at[y], s_z.at[j], r_z.at[0], (x, z, dest, c)).wait_send()
            for k, (lo, hi) in enumerate(CHUNKS):
                piece = pl.ds(lo * COLS, (hi - lo) * COLS)
                rcopy(part.at[j, piece], rsb.at[y, piece], s_rs.at[j, k], r_rs.at[0, k], (x, z, dest, c)).wait_send()
    for dp in range(NX):
        for dc in range(NC):
            p, cd = lax.rem(x + dp, NX), lax.rem(c + dc, NC)
            me = jnp.logical_and(diag, dp == 0 and dc == 0)

            @pl.when(jnp.logical_not(me))
            def _():
                rcopy(hb_snd.at[p, cd], hb_rcv.at[2 * y + c], s_hb.at[2 * dp + dc], r_hb.at[2 * y + c], (p, z, x, cd)).wait_send()


def body(ctx, resid, w, a, b, d, u, gain, lengths):
    vmem = pl.BlockSpec(memory_space=pltpu.VMEM)
    dma = lambda *n: pltpu.SemaphoreType.DMA(n)
    return pl.pallas_call(
        kernel,
        out_shape=(jax.ShapeDtypeStruct((10, RANK), F32), jax.ShapeDtypeStruct((1, HALF), F32)),
        in_specs=[vmem] * 8 + [pl.BlockSpec(memory_space=pltpu.SMEM)],
        out_specs=(vmem, vmem),
        scratch_shapes=[
            pltpu.VMEM((NX, NC, SEQ, HALF), BF),
            pltpu.VMEM((NC, NZ, COLS, HALF), BF),
            pltpu.VMEM((NC, 2 * RANK, HALF), BF),
            pltpu.VMEM((2, HALF + 16, SEQ), BF),
            pltpu.VMEM((2, HALF + 16, SEQ), BF),
            pltpu.VMEM((NC, HALF, SEQ), BF),
            pltpu.VMEM((NC, 8, SEQ), F32),
            pltpu.VMEM((NX, FEATS, SEQ), BF),
            pltpu.VMEM((NY, FEATS, SEQ), BF),
            pltpu.VMEM((NX, SEQ, SEQ), F32),
            pltpu.VMEM((NY, SEQ, SEQ), F32),
            pltpu.VMEM((FEATS, SEQ), F32),
            pltpu.VMEM((FEATS, SEQ), F32),
            pltpu.VMEM((FEATS, SEQ), F32),
            pltpu.VMEM((16, SEQ), F32),
            pltpu.VMEM((NX, 16, SEQ), F32),
            pltpu.VMEM((NX, RANK, SEQ), F32),
            pltpu.VMEM((NX, NC, COLS, SEQ), F32),
            pltpu.VMEM((8, COLS, SEQ), F32),
            pltpu.VMEM((NX, NC, 16, HALF), F32),
            pltpu.VMEM((8, 16, HALF), F32),
            pltpu.VMEM((COLS, SEQ), F32),
            pltpu.VMEM((16, HALF), F32),
            pltpu.VMEM((NZ, 16, SEQ), F32),
            pltpu.VMEM((NZ, 16, SEQ), F32),
            dma(7), dma(7), dma(16), dma(16), dma(16), dma(16), dma(1), dma(1), dma(2), dma(2), dma(8), dma(4),
            dma(NX, NCH), dma(NY, NCH), dma(NX), dma(NY), dma(NX), dma(NX), dma(NY), dma(NY), dma(8), dma(8),
            dma(8), dma(8), dma(NZ), dma(NZ),
        ],
        compiler_params=pltpu.CompilerParams(collective_id=0, has_side_effects=True, vmem_limit_bytes=40 << 20),
        cost_estimate=pl.CostEstimate(flops=2 * 1280 * 1280 * 512, bytes_accessed=2 << 20, transcendentals=0),
        name="hvp",
    )(ctx, resid, w.T, a.T, d.T, b, u, gain.reshape(5, SEQ), lengths)


def solution(mesh):
    grid = Mesh(mesh.devices.reshape(NX, NZ, NY, NC), AXES)
    dp, tensor = ("x", "z"), ("y", "c")
    in_specs = (
        P(dp, tensor),
        P(dp, tensor),
        P(tensor, dp),
        P(tensor, None),
        P(None, tensor),
        P(tensor, None),
        P(None, tensor),
        P(tensor),
        P(dp),
    )
    out_specs = (P(("y", "c", "x", "z"), None), P(dp, tensor))
    return jax.shard_map(body, mesh=grid, in_specs=in_specs, out_specs=out_specs, check_vma=False)
```

```python
import functools

import jax
import jax.numpy as jnp
from jax import lax
from jax.experimental import pallas as pl
from jax.experimental.pallas import tpu as pltpu
from jax.sharding import Mesh, PartitionSpec as P

AXES = ("x", "z", "y", "c")
NX, NZ, NY, NC = 4, 16, 4, 2
SEQ = 128
RANK = 64
FEATS = 1280
HALF = 640
COLS = 80
TOKENS = 16384
WIDTH = 5120
BF = jnp.bfloat16
F32 = jnp.float32
CHUNKS = ((0, 1),) + tuple((2 * s - 1, 2 * s + 1) for s in range(1, 8)) + ((15, 16),)
PARTS = ((0, 48), (48, 32))
NCH = len(CHUNKS)
NT = (((1,), (1,)), ((), ()))
TN = (((0,), (0,)), ((), ()))


def split2(v):
    hi = v.astype(BF)
    lo = (v - hi.astype(F32)).astype(BF)
    return hi, lo


def split3(v):
    hi = v.astype(BF)
    rest = v - hi.astype(F32)
    mid = rest.astype(BF)
    lo = (rest - mid.astype(F32)).astype(BF)
    return hi, mid, lo


def dot(a, b, dims=(((1,), (0,)), ((), ()))):
    return lax.dot_general(a, b, dims, preferred_element_type=F32)


def kernel(
    ctx_ref, resid_ref, wt_ref, at_ref, dt_ref, b_ref, u_ref, g_ref, len_ref,
    out_a, out_b,
    ctx_v, resid_v, bu_v, g_v, len_v,
    ctxs, ctxg, wg, adg, rt, relay, rrecv, buT, gr, part, rsb, zp, zr, zsum, zall, h_ref, dh_ref, gh_ref,
    st_snd, st_rcv, qg, ha_snd, ha_rcv, hb_snd, hb_sib, hb_red, hb_rcv, ha_sum, hb2, hbz, ha2, haz,
    s_in, s_ctx, r_ctx, s_w, r_w, s_ws, r_ws, s_ad, r_ad, s_res, r_res, s_rel, r_rel, s_bu, r_bu, s_rs, r_rs,
    s_zr, r_zr, s_zd, r_zd, s_st, r_st, s_q, r_q, s_ha, r_ha, s_hs, r_hs, s_hb, r_hb, s_bz, r_bz, s_az, r_az,
):
    x, z, y, c = [lax.axis_index(a) for a in AXES]
    other = lax.rem(c + 1, NC)
    diag = x == y

    def mod4(v):
        return lax.rem(v + 8, 4)

    def dev(dx=0, dz=0, dy=0, dc=0):
        return (mod4(x + dx), lax.rem(z + dz + NZ, NZ), mod4(y + dy), lax.rem(c + dc, NC))

    def rcopy(src, dst, ss, rs, to):
        return pltpu.make_async_remote_copy(
            src_ref=src, dst_ref=dst, send_sem=ss, recv_sem=rs, device_id=to, device_id_type=pl.DeviceIdType.MESH
        )

    def arrived(dst, rs):
        rcopy(dst, dst, s_ad.at[0], rs, dev(0, 0, 0, 1)).wait_recv()

    pending = []

    def send(src, dst, ss, rs, to):
        cp = rcopy(src, dst, ss, rs, to)
        cp.start()
        pending.append((None, cp))

    def send_unless(cond, src, dst, ss, rs, to):
        cp = rcopy(src, dst, ss, rs, to)
        keep = jnp.logical_not(cond)

        @pl.when(keep)
        def _():
            cp.start()

        pending.append((keep, cp))

    loads = [
        pltpu.make_async_copy(src, dst, s_in.at[i])
        for i, (src, dst) in enumerate((
            (wt_ref, wg.at[c, 0]),
            (ctx_ref, ctx_v),
            (at_ref, adg.at[c, pl.ds(0, RANK)]),
            (dt_ref, adg.at[c, pl.ds(RANK, RANK)]),
            (resid_ref, resid_v),
            (b_ref, bu_v.at[pl.ds(0, RANK)]),
            (u_ref, bu_v.at[pl.ds(RANK, RANK)]),
            (g_ref, g_v),
            (len_ref, len_v),
        ))
    ]
    for cp in loads:
        cp.start()

    barrier = pltpu.get_barrier_semaphore()
    count = 0
    for dx in range(NX):
        for dy in range(NY):
            for dc in range(NC):
                if (dx, dy, dc) != (0, 0, 0):
                    pl.semaphore_signal(barrier, inc=1, device_id=dev(dx, 0, dy, dc), device_id_type=pl.DeviceIdType.MESH)
                    count += 1
    for dz in range(1, NZ):
        pl.semaphore_signal(barrier, inc=1, device_id=dev(0, dz), device_id_type=pl.DeviceIdType.MESH)
        count += 1
    loads[1].wait()
    for half in range(2):
        ctxs[half] = ctx_v[half * SEQ:(half + 1) * SEQ, :].T
    loads[0].wait()
    pl.semaphore_wait(barrier, count)

    def w_copy(s, flow, sub):
        if s == 8:
            src, dst = 13 + flow, 15
        else:
            src, dst = (0 if s == 1 else 2 * s - 3 + flow), 2 * s - 1 + flow
        rows = pl.ds(*PARTS[sub])
        k = 4 * (s - 1) + 2 * flow + sub
        return rcopy(wg.at[c, src, rows], wg.at[c, dst, rows], s_w.at[k], r_w.at[k], dev(0, 1 - 2 * flow))

    def w_start(s, flow, sub):
        cp = w_copy(s, flow, sub)
        cp.start()
        pending.append((None, cp))

    def w_sib(slot):
        send(wg.at[c, slot], wg.at[c, slot], s_ws.at[slot], r_ws.at[slot], dev(0, 0, 0, 1))

    for sub in range(2):
        for flow in range(2):
            w_start(1, flow, sub)
    for half in range(2):
        for k, dx in ((1, 1), (3, -1)):
            send(ctxs.at[half], ctxg.at[x, c], s_ctx.at[k - 1 + half], r_ctx.at[k + c], (mod4(x + dx), z, y, half))
    send(ctxs.at[other], ctxg.at[x, c], s_ctx.at[4], r_ctx.at[0], dev(0, 0, 0, 1))
    w_sib(0)
    loads[2].wait()
    loads[3].wait()
    send(adg.at[c], adg.at[c], s_ad.at[0], r_ad.at[0], dev(0, 0, 0, 1))
    ctxg[x, c] = ctxs[c]

    loads[4].wait()
    loads[8].wait()
    lane = lax.broadcasted_iota(jnp.int32, (16, SEQ), 1)
    kq = y // 2
    for half in range(2):
        rt[half, 0:HALF] = resid_v[half * SEQ:(half + 1) * SEQ, :].T
        rt[half, HALF:] = jnp.where(lane < len_v[half], 1.0, 0.0).astype(BF)
        mine = jnp.logical_and(diag, c == half)
        send_unless(mine, rt.at[half], relay.at[kq, c], s_res.at[half], r_res.at[kq, c], (x, z, mod4(2 * y - x), half))

        @pl.when(mine)
        def _():
            relay[kq, c] = rt[half]

    for i in (5, 6, 7):
        loads[i].wait()
    off = jnp.logical_not(diag)

    @pl.when(diag)
    def _():
        buT[c] = bu_v[...].T
        gr[c] = jnp.concatenate([g_v[...], jnp.zeros((3, SEQ), F32)], axis=0)

    for dy in range(1, NY):
        send_unless(off, buT.at[c], buT.at[c], s_bu.at[dy - 1], r_bu.at[0], dev(0, 0, dy))
        send_unless(off, gr.at[c], gr.at[c], s_bu.at[dy + 2], r_bu.at[1], dev(0, 0, dy))

    def block(j):
        return mod4(x + j)

    def mm(js, k):
        lo, hi = CHUNKS[k]
        rows = (hi - lo) * COLS
        rhs = [jnp.concatenate([ctxg[block(j), cc] for j in js], axis=1) for cc in range(2)]
        lhs = [wg[cc, lo:hi].reshape(rows, HALF) for cc in range(2)]
        out = (dot(lhs[0], rhs[0]) + dot(lhs[1], rhs[1])).astype(BF)
        piece = pl.ds(lo * COLS, rows)
        for i, j in enumerate(js):
            part[j, piece] = out[:, i * SEQ:(i + 1) * SEQ]
            dest = mod4(x - j)
            send_unless(
                dest == y, part.at[j, piece], rsb.at[y, piece], s_rs.at[j, k], r_rs.at[mod4(dest - y), k], (x, z, dest, c)
            )

    def w_take(s, sub):
        for flow in range(2):
            if s < 8 or flow == sub:
                w_copy(s, flow, sub).wait_recv()
                if s < 7 or (s == 7 and flow == sub):
                    w_start(s + 1, flow, sub)
        if sub == 1:
            for slot in range(2 * s - 1, min(2 * s + 1, NZ)):
                w_sib(slot)

    def sib_wait(k):
        for slot in range(*CHUNKS[k]):
            arrived(wg.at[c, slot], r_ws.at[slot])

    def ctx_forward(i, dx_src, half_c, to_dx, sem):
        blk = ctxg.at[mod4(x + dx_src), half_c]
        send(blk, blk, s_ctx.at[sem], r_ctx.at[i], dev(to_dx))

    def ctx_wait(i):
        arrived(ctxg.at[0, 0], r_ctx.at[i])

    w_take(1, 0)
    ctx_wait(0)
    arrived(adg.at[c], r_ad.at[0])
    w_take(1, 1)
    zp[...] = dot(adg[0], ctxg[x, 0]) + dot(adg[1], ctxg[x, 1])
    zp_rows = lambda yy: zp.at[pl.ds(pl.multiple_of(yy * 32, 32), 32)]
    for dy in range(1, NY):
        yd = mod4(y + dy)
        send(zp_rows(yd), zr.at[dy], s_zr.at[dy], r_zr.at[dy], dev(0, 0, dy))
    sib_wait(0)
    mm((0,), 0)
    w_take(2, 0)
    w_take(2, 1)
    sib_wait(1)
    mm((0,), 1)
    w_take(3, 0)
    w_take(3, 1)
    sib_wait(2)
    mm((0,), 2)
    ctx_wait(1)
    ctx_forward(5, -1, 0, 1, 5)
    ctx_wait(4)
    ctx_forward(6, 1, 1, -1, 6)
    ctx_wait(2)
    ctx_wait(3)
    mm((1, 3), 0)
    mm((1, 3), 1)
    mm((1, 3), 2)
    w_take(4, 0)
    w_take(4, 1)
    sib_wait(3)
    mm((0, 1, 3), 3)
    acc = zp[pl.ds(pl.multiple_of(y * 32, 32), 32)]
    for dy in range(1, NY):
        arrived(zr.at[dy], r_zr.at[dy])
        acc = acc + zr[dy]
    zsum[...] = acc
    for dq in range(NX):
        me = jnp.logical_and(diag, dq == 0)
        send_unless(me, zsum, zall.at[y], s_zd.at[dq], r_zd.at[y], (mod4(x + dq), z, mod4(x + 2 * dq), c))

    @pl.when(diag)
    def _():
        zall[y] = acc

    w_take(5, 0)
    w_take(5, 1)
    sib_wait(4)
    mm((0, 1, 3), 4)
    is_relay = (x + y) % 2 == 0
    q0 = lax.rem((x + y) // 2, 2)
    for k in range(2):
        q = q0 + 2 * k
        for cc in range(2):
            own = jnp.logical_and(diag, jnp.logical_and(kq == k, c == cc))
            here = jnp.logical_and(is_relay, jnp.logical_not(own))

            @pl.when(here)
            def _():
                arrived(relay.at[k, cc], r_res.at[k, cc])

            stay = q == x
            send_unless(
                jnp.logical_not(jnp.logical_and(is_relay, q != x)),
                relay.at[k, cc], rrecv.at[cc], s_rel.at[k, cc], r_rel.at[cc], (q, z, y, c),
            )

            @pl.when(jnp.logical_and(is_relay, stay))
            def _():
                rrecv[cc] = relay[k, cc]

    ctx_wait(5)
    ctx_wait(6)
    mm((2,), 0)
    mm((2,), 1)
    mm((2,), 2)
    w_take(6, 0)
    w_take(6, 1)
    mm((2,), 3)
    mm((2,), 4)
    sib_wait(5)
    mm((0, 1, 2, 3), 5)

    @pl.when(off)
    def _():
        arrived(buT.at[c], r_bu.at[0])
        arrived(gr.at[c], r_bu.at[1])

    send(buT.at[c], buT.at[c], s_bu.at[6], r_bu.at[2], dev(0, 0, 0, 1))
    send(gr.at[c], gr.at[c], s_bu.at[7], r_bu.at[3], dev(0, 0, 0, 1))
    w_take(7, 0)
    w_take(7, 1)
    sib_wait(6)
    mm((0, 1, 2, 3), 6)
    w_take(8, 0)
    w_take(8, 1)
    sib_wait(7)
    mm((0, 1, 2, 3), 7)
    sib_wait(8)
    mm((0, 1, 2, 3), 8)

    for ys in range(NY):
        @pl.when(jnp.logical_not(jnp.logical_and(diag, y == ys)))
        def _():
            arrived(zall.at[ys], r_zd.at[ys])

    arrived(buT.at[c], r_bu.at[2])
    arrived(gr.at[c], r_bu.at[3])
    zt = jnp.concatenate([zall[0], zall[1]], axis=0)
    ztt = jnp.concatenate([zall[2], zall[3]], axis=0)
    zero = jnp.zeros((RANK, SEQ), F32)
    rhs = jnp.concatenate([jnp.concatenate([ztt, zt], axis=0), jnp.concatenate([zt, zero], axis=0)], axis=1)
    r1, r2, r3 = split3(rhs)
    for cc in range(2):
        m = buT[cc]
        both = dot(m, r1) + dot(m, r2) + dot(m, r3)
        dh_ref[cc * HALF:(cc + 1) * HALF] = both[:, 0:SEQ]
        h_ref[cc * HALF:(cc + 1) * HALF] = both[:, SEQ:]

    for cc in range(2):
        @pl.when(off)
        def _():
            arrived(rrecv.at[cc], r_rel.at[cc])
        h_ref[cc * HALF:(cc + 1) * HALF] = h_ref[cc * HALF:(cc + 1) * HALF] + rrecv[cc, 0:HALF].astype(F32)
    live = rrecv[0, HALF:].astype(F32)[0:1] * (1.0 / jnp.sqrt(jnp.float32(TOKENS)))

    jown = mod4(x - y)
    for k, (lo, hi) in enumerate(CHUNKS):
        for dy in range(1, NY):
            piece = pl.ds(lo * COLS, (hi - lo) * COLS)
            arrived(rsb.at[mod4(y - dy), piece], r_rs.at[dy, k])
        for slot in range(lo, hi):
            step = (slot + 1) // 2
            zz = z if slot == 0 else (z - step if slot % 2 == 1 else z + step)
            zz = lax.rem(zz + NZ, NZ)
            rows = pl.ds(pl.multiple_of(zz * COLS, 16), COLS)
            piece = pl.ds(slot * COLS, COLS)
            acc = part[jown, piece].astype(F32)
            for dy in range(1, NY):
                acc = acc + rsb[mod4(y - dy), piece].astype(F32)
            h_ref[rows] = h_ref[rows] + acc

    def gsq(i):
        row = gr[i // 5, pl.ds(i % 5, 1)]
        col = jnp.broadcast_to(row, (SEQ, SEQ)).T
        return col * col

    sums = [jnp.zeros((8, SEQ), F32) for _ in range(9)]

    def fold(v):
        return jnp.sum(v.reshape(16, 8, SEQ), axis=0)

    for i in range(10):
        rows = pl.ds(i * SEQ, SEQ)
        h = h_ref[rows]
        d = dh_ref[rows]
        g2 = gsq(i)
        gh_ref[rows] = g2
        hd = h * d
        hh = h * h
        terms = (h, hh, d, hd, g2 * d, g2, g2 * h, g2 * hh, g2 * hd)
        sums = [s + fold(t) for s, t in zip(sums, terms)]
    for n, s in enumerate(sums):
        st_snd[n:n + 1] = jnp.sum(s, axis=0, keepdims=True)
    st_snd[9:] = jnp.zeros((7, SEQ), F32)
    for dx in range(1, NX):
        send(st_snd, st_rcv.at[dx], s_st.at[dx], r_st.at[dx], (mod4(x + dx), z, mod4(y + 2 * dx), c))
    total = st_snd[...]
    for dx in range(1, NX):
        arrived(st_rcv.at[dx], r_st.at[dx])
        total = total + st_rcv[dx]
    total = total * (1.0 / WIDTH)
    mu, e_hh, m1, e_hd, e_gd, e_g, e_gh, e_ghh, e_ghd = [total[n:n + 1] for n in range(9)]
    rinv = lax.rsqrt(e_hh - mu * mu + 1e-05)
    m2 = rinv * (e_hd - mu * m1)
    g_n = rinv * (e_gh - mu * e_g)
    g_nn = rinv * rinv * (e_ghh - 2.0 * mu * e_gh + mu * mu * e_g)
    g_nd = rinv * (e_ghd - mu * e_gd)
    lr = live * rinv
    m3 = lr * (e_gd - m1 * e_g - m2 * g_n)
    m4 = lr * (g_nd - m1 * g_n - m2 * g_nn)

    q = jnp.zeros((SEQ, 2 * SEQ), F32)
    parts = []
    for cc in range(2):
        rows = pl.ds(cc * HALF, HALF)
        n = (h_ref[rows] - mu) * rinv
        cot = lr * gh_ref[rows] * (dh_ref[rows] - m1 - n * m2)
        g1, g2 = split2(rinv * (cot - m3 - n * m4))
        parts.append((g1, g2))
        q = q + dot(buT[cc], jnp.concatenate([g1, g2], axis=1), TN)
    xq = mod4(2 * x - y)
    q1, q2 = split2(q[0:RANK, 0:SEQ] + q[0:RANK, SEQ:])
    qg[xq] = jnp.concatenate([q1, q2], axis=0).T
    for dy in range(1, NY):
        send(qg.at[xq], qg.at[xq], s_q.at[dy], r_q.at[dy], dev(0, 0, dy))

    z1, z2 = split2(zt)
    zs = jnp.concatenate([z1, z2], axis=0)
    for cc in range(2):
        g1, g2 = parts[cc]
        hb = dot(zs, g1, NT) + dot(zs, g2, NT)
        hb = hb[0:RANK] + hb[RANK:]
        for p in range(NX):
            hb_snd[cc, p] = hb[16 * p:16 * (p + 1)]
    send(hb_snd.at[other], hb_sib, s_hs.at[0], r_hs.at[0], dev(0, 0, 0, 1))
    arrived(hb_sib, r_hs.at[0])
    hb_red[...] = hb_snd[c] + hb_sib[...]
    for dp in range(NX):
        p = mod4(x + dp)
        me = jnp.logical_and(diag, dp == 0)
        send_unless(me, hb_red.at[p], hb_rcv.at[y], s_hb.at[dp], r_hb.at[y], (p, z, x, c))

    @pl.when(diag)
    def _():
        hb_rcv[y] = hb_red[x]

    for dy in range(1, NY):
        arrived(qg.at[xq], r_q.at[dy])
    qs = jnp.concatenate([qg[xb] for xb in range(NX)], axis=0)
    low = lax.broadcasted_iota(jnp.int32, (COLS, SEQ), 1) < RANK
    for cc in range(2):
        t = dot(jnp.concatenate([ctxg[xb, cc] for xb in range(NX)], axis=1), qs)
        t = t + pltpu.roll(t, RANK, 1)
        for p in range(NX):
            ha_snd[p, cc] = jnp.where(low, t[160 * p:160 * p + COLS], t[160 * p + COLS:160 * (p + 1)])
    for dx in range(NX):
        for dc in range(NC):
            if (dx, dc) != (0, 0):
                p, cd = mod4(x + dx), lax.rem(c + dc, NC)
                i = 2 * dx + dc
                send(ha_snd.at[p, cd], ha_rcv.at[i], s_ha.at[i], r_ha.at[i], (p, z, y, cd))
    for ys in range(NY):
        @pl.when(jnp.logical_not(jnp.logical_and(diag, y == ys)))
        def _():
            arrived(hb_rcv.at[ys], r_hb.at[ys])
    acc = hb_rcv[0] + hb_rcv[1] + hb_rcv[2] + hb_rcv[3]
    for k in range(5):
        tile = acc[:, k * SEQ:(k + 1) * SEQ]
        for zi in range(NZ):
            hb2[zi, k:k + 1] = tile[zi:zi + 1]
    for dz in range(1, NZ):
        send(hb2.at[lax.rem(z + dz, NZ)], hbz.at[dz], s_bz.at[dz], r_bz.at[dz], dev(0, dz))
    acc = ha_snd[x, c]
    for i in range(1, 8):
        arrived(ha_rcv.at[i], r_ha.at[i])
        acc = acc + ha_rcv[i]
    ha_sum[...] = acc
    low = lax.broadcasted_iota(jnp.int32, (8, SEQ), 1) < RANK
    for k in range(5):
        a = ha_sum[pl.ds(k, 8, stride=10)]
        b = ha_sum[pl.ds(k + 5, 8, stride=10)]
        v = jnp.where(low, a, pltpu.roll(b, RANK, 1))
        w = jnp.where(low, pltpu.roll(a, RANK, 1), b)
        for zi in range(8):
            ha2[zi, k:k + 1] = v[zi:zi + 1]
            ha2[zi + 8, k:k + 1] = w[zi:zi + 1]
    for dz in range(1, NZ):
        send(ha2.at[lax.rem(z + dz, NZ)], haz.at[dz], s_az.at[dz], r_az.at[dz], dev(0, dz))
    acc = hb2[z]
    for dz in range(1, NZ):
        arrived(hbz.at[dz], r_bz.at[dz])
        acc = acc + hbz[dz]
    for k in range(5):
        out_b[0:1, k * SEQ:(k + 1) * SEQ] = acc[k:k + 1]
    acc = ha2[z]
    for dz in range(1, NZ):
        arrived(haz.at[dz], r_az.at[dz])
        acc = acc + haz[dz]
    out_a[0:5] = acc[0:5, 0:RANK]
    out_a[5:10] = acc[0:5, RANK:]

    for keep, cp in pending:
        if keep is None:
            cp.wait_send()
        else:
            @pl.when(keep)
            def _():
                cp.wait_send()


def body(ctx, resid, w, a, b, d, u, gain, lengths):
    vmem = pl.BlockSpec(memory_space=pltpu.VMEM)
    dma = lambda *n: pltpu.SemaphoreType.DMA(n)
    return pl.pallas_call(
        kernel,
        out_shape=(jax.ShapeDtypeStruct((10, RANK), F32), jax.ShapeDtypeStruct((1, HALF), F32)),
        in_specs=[pl.BlockSpec(memory_space=pl.ANY)] * 9,
        out_specs=(vmem, vmem),
        scratch_shapes=[
            pltpu.VMEM((2 * SEQ, HALF), BF),
            pltpu.VMEM((2 * SEQ, HALF), BF),
            pltpu.VMEM((2 * RANK, HALF), BF),
            pltpu.VMEM((5, SEQ), F32),
            pltpu.SMEM((2,), jnp.int32),
            pltpu.VMEM((2, HALF, SEQ), BF),
            pltpu.VMEM((NX, NC, HALF, SEQ), BF),
            pltpu.VMEM((NC, NZ, COLS, HALF), BF),
            pltpu.VMEM((NC, 2 * RANK, HALF), BF),
            pltpu.VMEM((2, HALF + 16, SEQ), BF),
            pltpu.VMEM((2, 2, HALF + 16, SEQ), BF),
            pltpu.VMEM((2, HALF + 16, SEQ), BF),
            pltpu.VMEM((NC, HALF, SEQ), BF),
            pltpu.VMEM((NC, 8, SEQ), F32),
            pltpu.VMEM((NX, FEATS, SEQ), BF),
            pltpu.VMEM((NY, FEATS, SEQ), BF),
            pltpu.VMEM((SEQ, SEQ), F32),
            pltpu.VMEM((NY, 32, SEQ), F32),
            pltpu.VMEM((32, SEQ), F32),
            pltpu.VMEM((NY, 32, SEQ), F32),
            pltpu.VMEM((FEATS, SEQ), F32),
            pltpu.VMEM((FEATS, SEQ), F32),
            pltpu.VMEM((FEATS, SEQ), F32),
            pltpu.VMEM((16, SEQ), F32),
            pltpu.VMEM((NX, 16, SEQ), F32),
            pltpu.VMEM((NX, SEQ, SEQ), BF),
            pltpu.VMEM((NX, NC, COLS, SEQ), F32),
            pltpu.VMEM((8, COLS, SEQ), F32),
            pltpu.VMEM((NC, NX, 16, HALF), F32),
            pltpu.VMEM((NX, 16, HALF), F32),
            pltpu.VMEM((NX, 16, HALF), F32),
            pltpu.VMEM((NY, 16, HALF), F32),
            pltpu.VMEM((COLS, SEQ), F32),
            pltpu.VMEM((NZ, 8, SEQ), F32),
            pltpu.VMEM((NZ, 8, SEQ), F32),
            pltpu.VMEM((NZ, 8, SEQ), F32),
            pltpu.VMEM((NZ, 8, SEQ), F32),
            dma(9),
            dma(7), dma(7), dma(32), dma(32), dma(16), dma(16), dma(1), dma(1), dma(2), dma(2, 2), dma(2, 2), dma(2),
            dma(8), dma(4), dma(NX, NCH), dma(NY, NCH),
            dma(NY), dma(NY), dma(NX), dma(NY), dma(NX), dma(NX), dma(NY), dma(NY), dma(8), dma(8), dma(1), dma(1),
            dma(NX), dma(NY), dma(NZ), dma(NZ), dma(NZ), dma(NZ),
        ],
        compiler_params=pltpu.CompilerParams(collective_id=0, has_side_effects=True, vmem_limit_bytes=40 << 20),
        cost_estimate=pl.CostEstimate(flops=2 * 1280 * 1280 * 512, bytes_accessed=2 << 20, transcendentals=0),
        name="hvp",
    )(ctx, resid, w.T, a.T, d.T, b, u, gain.reshape(5, SEQ), lengths)


def solution(mesh):
    grid = Mesh(mesh.devices.reshape(NX, NZ, NY, NC), AXES)
    dp, tensor = ("x", "z"), ("y", "c")
    in_specs = (
        P(dp, tensor),
        P(dp, tensor),
        P(tensor, dp),
        P(tensor, None),
        P(None, tensor),
        P(tensor, None),
        P(None, tensor),
        P(tensor),
        P(dp),
    )
    out_specs = (P(("y", "c", "x", "z"), None), P(dp, tensor))
    return jax.shard_map(body, mesh=grid, in_specs=in_specs, out_specs=out_specs, check_vma=False)
```

```python
import functools

import jax
import jax.numpy as jnp
from jax import lax
from jax.experimental import pallas as pl
from jax.experimental.pallas import tpu as pltpu
from jax.sharding import Mesh, PartitionSpec as P

AXES = ("x", "z", "y", "c")
NX, NZ, NY, NC = 4, 16, 4, 2
SEQ = 128
RANK = 64
FEATS = 1280
HALF = 640
COLS = 80
TOKENS = 16384
WIDTH = 5120
BF = jnp.bfloat16
F32 = jnp.float32
CHUNKS = ((0, 1),) + tuple((2 * s - 1, 2 * s + 1) for s in range(1, 8)) + ((15, 16),)
PARTS = ((0, 32), (32, 32), (64, 16))
NP = len(PARTS)
NCH = len(CHUNKS)
NT = (((1,), (1,)), ((), ()))
TN = (((0,), (0,)), ((), ()))


def split2(v):
    hi = v.astype(BF)
    lo = (v - hi.astype(F32)).astype(BF)
    return hi, lo


def split3(v):
    hi = v.astype(BF)
    rest = v - hi.astype(F32)
    mid = rest.astype(BF)
    lo = (rest - mid.astype(F32)).astype(BF)
    return hi, mid, lo


def dot(a, b, dims=(((1,), (0,)), ((), ()))):
    return lax.dot_general(a, b, dims, preferred_element_type=F32)


def kernel(
    ctx_ref, resid_ref, wt_ref, at_ref, dt_ref, b_ref, u_ref, g_ref, len_ref,
    out_a, out_b,
    ctx_v, resid_v, bu_v, g_v, len_v,
    ctxs, ctxg, wg, adg, rt, relay, rrecv, buT, gr, part, rsb, zp, zr, zsum, zall, es, ls, h_ref, dh_ref, gh_ref,
    qg, ha_snd, ha_sib, hb_snd, hb_sib, hb_red, hb_rcv, ha_sum, hb2, hbz, ha2, haz,
    s_in, s_ctx, r_ctx, s_w, r_w, s_ws, r_ws, s_ad, r_ad, s_res, r_res, s_rel, r_rel, s_bu, r_bu, s_rs, r_rs,
    s_zr, r_zr, s_zd, r_zd, s_es, r_es, s_st, r_st, s_q, r_q, s_ha, r_ha, s_hs, r_hs, s_hb, r_hb, s_bz, r_bz, s_az, r_az,
):
    x, z, y, c = [lax.axis_index(a) for a in AXES]
    other = lax.rem(c + 1, NC)
    diag = x == y

    def mod4(v):
        return lax.rem(v + 8, 4)

    def dev(dx=0, dz=0, dy=0, dc=0):
        return (mod4(x + dx), lax.rem(z + dz + NZ, NZ), mod4(y + dy), lax.rem(c + dc, NC))

    def rcopy(src, dst, ss, rs, to):
        return pltpu.make_async_remote_copy(
            src_ref=src, dst_ref=dst, send_sem=ss, recv_sem=rs, device_id=to, device_id_type=pl.DeviceIdType.MESH
        )

    def arrived(dst, rs):
        rcopy(dst, dst, s_ad.at[0], rs, dev(0, 0, 0, 1)).wait_recv()

    pending = []

    def send(src, dst, ss, rs, to):
        cp = rcopy(src, dst, ss, rs, to)
        cp.start()
        pending.append((None, cp))

    def send_unless(cond, src, dst, ss, rs, to):
        cp = rcopy(src, dst, ss, rs, to)
        keep = jnp.logical_not(cond)

        @pl.when(keep)
        def _():
            cp.start()

        pending.append((keep, cp))

    loads = [
        pltpu.make_async_copy(src, dst, s_in.at[i])
        for i, (src, dst) in enumerate((
            (wt_ref, wg.at[c, 0]),
            (ctx_ref, ctx_v),
            (at_ref, adg.at[c, pl.ds(0, RANK)]),
            (dt_ref, adg.at[c, pl.ds(RANK, RANK)]),
            (resid_ref, resid_v),
            (b_ref, bu_v.at[pl.ds(0, RANK)]),
            (u_ref, bu_v.at[pl.ds(RANK, RANK)]),
            (g_ref, g_v),
            (len_ref, len_v),
        ))
    ]
    for cp in loads:
        cp.start()

    barrier = pltpu.get_barrier_semaphore()
    count = 0
    for dx in range(NX):
        for dy in range(NY):
            for dc in range(NC):
                if (dx, dy, dc) != (0, 0, 0):
                    pl.semaphore_signal(barrier, inc=1, device_id=dev(dx, 0, dy, dc), device_id_type=pl.DeviceIdType.MESH)
                    count += 1
    for dz in (-1, 1):
        pl.semaphore_signal(barrier, inc=1, device_id=dev(0, dz), device_id_type=pl.DeviceIdType.MESH)
        count += 1
    pl.semaphore_wait(barrier, count)

    def w_copy(s, flow, sub):
        if s == 8:
            src, dst = 13 + flow, 15
        else:
            src, dst = (0 if s == 1 else 2 * s - 3 + flow), 2 * s - 1 + flow
        rows = pl.ds(*PARTS[sub])
        k = NP * (2 * (s - 1) + flow) + sub
        source = wt_ref.at[rows] if s == 1 else wg.at[c, src, rows]
        return rcopy(source, wg.at[c, dst, rows], s_w.at[k], r_w.at[k], dev(0, 1 - 2 * flow))

    def w_start(s, flow, sub):
        cp = w_copy(s, flow, sub)
        cp.start()
        pending.append((None, cp))

    def w_sib(slot):
        send(wg.at[c, slot], wg.at[c, slot], s_ws.at[slot], r_ws.at[slot], dev(0, 0, 0, 1))

    def first(sub):
        for flow in range(2):
            w_start(1, flow, sub)

    first(0)
    loads[1].wait()
    for half in range(2):
        ctxs[half] = ctx_v[half * SEQ:(half + 1) * SEQ, :].T
    lead = 1 - 2 * c
    ctx_sends_to = lambda which, dx, k: [
        send(ctxs.at[half], ctxg.at[x, c], s_ctx.at[2 * which + half], r_ctx.at[k], (mod4(x + dx), z, y, half))
        for half in range(2)
    ]
    ctx_sends_to(0, lead, jnp.where(c == 0, 1, 4))
    send(ctxs.at[other], ctxg.at[x, c], s_ctx.at[4], r_ctx.at[0], dev(0, 0, 0, 1))
    loads[0].wait()
    w_sib(0)
    loads[2].wait()
    loads[3].wait()
    send(adg.at[c], adg.at[c], s_ad.at[0], r_ad.at[0], dev(0, 0, 0, 1))
    ctxg[x, c] = ctxs[c]

    loads[4].wait()
    loads[8].wait()
    lane = lax.broadcasted_iota(jnp.int32, (16, SEQ), 1)
    off = jnp.logical_not(diag)
    for half in range(2):
        rt[half, 0:HALF] = resid_v[half * SEQ:(half + 1) * SEQ, :].T
        rt[half, HALF:] = jnp.where(lane < len_v[half], 1.0, 0.0).astype(BF)

        @pl.when(jnp.logical_and(diag, c == half))
        def _():
            rrecv[c] = rt[half]

    send_unless(diag, rt.at[0], relay.at[y, c], s_res.at[0], r_res.at[y, c], (x, z, x, 0))
    send_unless(jnp.logical_or(off, c == 0), rt.at[0], rrecv.at[c], s_res.at[0], r_rel.at[c], (x, z, x, 0))
    first(1)
    for i in (5, 6, 7):
        loads[i].wait()

    @pl.when(diag)
    def _():
        buT[c] = bu_v[...].T
        gr[c] = jnp.concatenate([g_v[...], jnp.zeros((3, SEQ), F32)], axis=0)

    for dy in range(1, NY):
        send_unless(off, buT.at[c], buT.at[c], s_bu.at[dy - 1], r_bu.at[0], dev(0, 0, dy))
        send_unless(off, gr.at[c], gr.at[c], s_bu.at[dy + 2], r_bu.at[1], dev(0, 0, dy))

    first(2)
    def block(j):
        return mod4(x + j)

    def mm(js, k):
        lo, hi = CHUNKS[k]
        rows = (hi - lo) * COLS
        rhs = [jnp.concatenate([ctxg[block(j), cc] for j in js], axis=1) for cc in range(2)]
        lhs = [wg[cc, lo:hi].reshape(rows, HALF) for cc in range(2)]
        out = (dot(lhs[0], rhs[0]) + dot(lhs[1], rhs[1])).astype(BF)
        piece = pl.ds(lo * COLS, rows)
        for i, j in enumerate(js):
            part[j, piece] = out[:, i * SEQ:(i + 1) * SEQ]
            dest = mod4(x + j)
            send_unless(
                dest == y, part.at[j, piece], rsb.at[y, piece], s_rs.at[j, k], r_rs.at[mod4(dest - y), k], (x, z, dest, c)
            )

    def last_hop(flow):
        return (0, 2) if flow == 0 else (1,)

    def w_take(s, sub):
        for flow in range(2):
            if s < 8 or sub in last_hop(flow):
                w_copy(s, flow, sub).wait_recv()
                if s < 7 or (s == 7 and sub in last_hop(flow)):
                    w_start(s + 1, flow, sub)
        if sub == NP - 1:
            for slot in range(2 * s - 1, min(2 * s + 1, NZ)):
                w_sib(slot)

    def sib_wait(k):
        for slot in range(*CHUNKS[k]):
            arrived(wg.at[c, slot], r_ws.at[slot])

    def ctx_forward(i, dx_src, half_c, to_dx, sem):
        blk = ctxg.at[mod4(x + dx_src), half_c]
        send(blk, blk, s_ctx.at[sem], r_ctx.at[i], dev(to_dx))

    def ctx_wait(i):
        arrived(ctxg.at[0, 0], r_ctx.at[i])

    def low_rank_sum():
        acc = zp[pl.ds(pl.multiple_of(y * 32, 32), 32)]
        for dy in range(1, NY):
            arrived(zr.at[dy], r_zr.at[dy])
            acc = acc + zr[dy]
        zsum[...] = acc
        for dq in range(NX):
            me = jnp.logical_and(diag, dq == 0)
            send_unless(me, zsum, zall.at[y], s_zd.at[dq], r_zd.at[y], (mod4(x + dq), z, x, c))

        @pl.when(diag)
        def _():
            zall[y] = acc

    def resid_half():
        send_unless(jnp.logical_and(diag, c == 1), rt.at[1], rrecv.at[c], s_res.at[1], r_rel.at[c], (y, z, x, 1))

    def second_leg():
        pass_on = jnp.logical_and(diag, c == 0)
        for dq in range(1, NX):
            q = mod4(x + dq)
            for cc in range(2):
                @pl.when(pass_on)
                def _():
                    arrived(relay.at[q, cc], r_res.at[q, cc])

                send_unless(
                    jnp.logical_not(pass_on), relay.at[q, cc], rrecv.at[cc], s_rel.at[dq, cc], r_rel.at[cc], (q, z, x, 0)
                )

    def adapter_on():
        @pl.when(off)
        def _():
            arrived(buT.at[c], r_bu.at[0])
            arrived(gr.at[c], r_bu.at[1])

        send(buT.at[c], buT.at[c], s_bu.at[6], r_bu.at[2], dev(0, 0, 0, 1))
        send(gr.at[c], gr.at[c], s_bu.at[7], r_bu.at[3], dev(0, 0, 0, 1))

    def hop(s, *work):
        for sub in range(NP):
            w_take(s, sub)
            for f in work[len(work) * sub // NP:len(work) * (sub + 1) // NP]:
                f()

    def zp_sum():
        ctx_wait(0)
        arrived(adg.at[c], r_ad.at[0])
        zp[...] = dot(adg[0], ctxg[x, 0]) + dot(adg[1], ctxg[x, 1])

    def zp_send():
        for dy in range(1, NY):
            rows = pl.ds(pl.multiple_of(mod4(y + dy) * 32, 32), 32)
            send(zp.at[rows], zr.at[dy], s_zr.at[dy], r_zr.at[dy], dev(0, 0, dy))

    def ctx_near():
        ctx_wait(2)
        ctx_wait(3)

    def ctx_pass():
        ctx_wait(1)
        ctx_forward(5, -1, 0, 1, 5)
        ctx_wait(4)
        ctx_forward(6, 1, 1, -1, 6)

    def ctx_far():
        ctx_wait(5)
        ctx_wait(6)

    def m(js, *ks):
        return lambda: [mm(js, k) for k in ks]

    def sw(k):
        return lambda: sib_wait(k)

    ctx_second = lambda: ctx_sends_to(1, -lead, jnp.where(c == 0, 3, 2))

    def low_rank_terms():
        for ys in range(NY):
            @pl.when(jnp.logical_not(jnp.logical_and(diag, y == ys)))
            def _():
                arrived(zall.at[ys], r_zd.at[ys])

        arrived(buT.at[c], r_bu.at[2])
        arrived(gr.at[c], r_bu.at[3])
        zt = jnp.concatenate([zall[0], zall[1]], axis=0)
        ztt = jnp.concatenate([zall[2], zall[3]], axis=0)
        zero = jnp.zeros((RANK, SEQ), F32)
        rhs = jnp.concatenate([jnp.concatenate([ztt, zt], axis=0), jnp.concatenate([zt, zero], axis=0)], axis=1)
        r1, r2, r3 = split3(rhs)
        for cc in range(2):
            b = buT[cc]
            both = dot(b, r1) + dot(b, r2) + dot(b, r3)
            dh_ref[cc * HALF:(cc + 1) * HALF] = both[:, 0:SEQ]
            h_ref[cc * HALF:(cc + 1) * HALF] = both[:, SEQ:]

    def fold(v):
        return jnp.sum(v.reshape(-1, 8, SEQ), axis=0)

    def early_sums():
        for i in range(10):
            col = jnp.broadcast_to(gr[i // 5, pl.ds(i % 5, 1)], (SEQ, SEQ)).T
            gh_ref[i * SEQ:(i + 1) * SEQ] = col * col
        acc = jnp.zeros((SEQ, 3 * SEQ), F32)
        sums = [jnp.zeros((8, SEQ), F32) for _ in range(3)]
        lane = lax.broadcasted_iota(jnp.int32, (HALF, SEQ), 1)
        for cc in range(2):
            rows = pl.ds(cc * HALF, HALF)
            g2 = gh_ref[rows]
            d = dh_ref[rows]
            gd = g2 * d
            d1, d2 = split2(gd)
            k1, k2 = split2(jnp.where(lane < RANK, 1.0, g2))
            acc = acc + dot(buT[cc], jnp.concatenate([d1, d2, k1], axis=1), TN)
            e2 = dot(buT[cc], k2, TN)
            acc = acc + jnp.concatenate([jnp.zeros((SEQ, 2 * SEQ), F32), e2], axis=1)
            sums = [s + fold(t) for s, t in zip(sums, (d, gd, g2))]
        es[0, 0:RANK] = acc[0:RANK, 0:SEQ] + acc[0:RANK, SEQ:2 * SEQ]
        es[0, RANK:2 * RANK] = acc[0:RANK, 2 * SEQ:]
        for n, s in enumerate(sums):
            es[0, 2 * RANK + n:2 * RANK + n + 1] = jnp.sum(s, axis=0, keepdims=True)
        es[0, 2 * RANK + 3:] = jnp.zeros((5, SEQ), F32)

    def early_send():
        for dx in range(1, NX):
            send(es.at[0], es.at[dx], s_es.at[dx], r_es.at[dx], (mod4(x + dx), z, y, c))

    hop(1, ctx_second, zp_sum, zp_send)
    hop(2, sw(0), m((0,), 0), lambda: None)
    hop(3, sw(1), m((0,), 1), ctx_pass)
    hop(4, sw(2), m((0,), 2), ctx_near, m((1, 3), 0), m((1, 3), 1), lambda: (low_rank_sum(), resid_half()))
    hop(5, m((1, 3), 2), sw(3), m((1, 3), 3), m((0,), 3), lambda: None, adapter_on)
    hop(6, sw(4), m((1, 3), 4), m((0,), 4), second_leg, ctx_far, m((2,), 0))
    hop(7, m((2,), 1, 2), m((2,), 3), sw(5), m((1, 3), 5), m((0,), 5), m((2,), 4, 5))
    hop(8, low_rank_terms, sw(6), m((1, 2), 6), m((0, 3), 6), early_sums, early_send)
    sib_wait(7)
    mm((0, 1, 2, 3), 7)
    sib_wait(8)
    mm((0, 1, 2, 3), 8)

    for cc in range(2):
        @pl.when(jnp.logical_not(jnp.logical_and(diag, c == cc)))
        def _():
            arrived(rrecv.at[cc], r_rel.at[cc])
        h_ref[cc * HALF:(cc + 1) * HALF] = h_ref[cc * HALF:(cc + 1) * HALF] + rrecv[cc, 0:HALF].astype(F32)
    live = rrecv[0, HALF:].astype(F32)[0:1] * (1.0 / jnp.sqrt(jnp.float32(TOKENS)))

    jown = mod4(y - x)
    for k, (lo, hi) in enumerate(CHUNKS):
        for dy in range(1, NY):
            piece = pl.ds(lo * COLS, (hi - lo) * COLS)
            arrived(rsb.at[mod4(y - dy), piece], r_rs.at[dy, k])
        for slot in range(lo, hi):
            step = (slot + 1) // 2
            zz = z if slot == 0 else (z - step if slot % 2 == 1 else z + step)
            zz = lax.rem(zz + NZ, NZ)
            rows = pl.ds(pl.multiple_of(zz * COLS, 16), COLS)
            piece = pl.ds(slot * COLS, COLS)
            acc = part[jown, piece].astype(F32)
            for dy in range(1, NY):
                acc = acc + rsb[mod4(y - dy), piece].astype(F32)
            h_ref[rows] = h_ref[rows] + acc

    acc = jnp.zeros((SEQ, 4 * SEQ), F32)
    sums = [jnp.zeros((8, SEQ), F32) for _ in range(6)]
    for cc in range(2):
        rows = pl.ds(cc * HALF, HALF)
        h = h_ref[rows]
        d = dh_ref[rows]
        g2 = gh_ref[rows]
        gh = g2 * h
        h1, h2 = split2(h)
        g1, g3 = split2(gh)
        acc = acc + dot(buT[cc], jnp.concatenate([h1, h2, g1, g3], axis=1), TN)
        sums = [s + fold(t) for s, t in zip(sums, (h, h * h, h * d, gh, gh * h, gh * d))]
    ls[0, 0:RANK] = acc[0:RANK, 0:SEQ] + acc[0:RANK, SEQ:2 * SEQ]
    ls[0, RANK:2 * RANK] = acc[0:RANK, 2 * SEQ:3 * SEQ] + acc[0:RANK, 3 * SEQ:]
    for n, s in enumerate(sums):
        ls[0, 2 * RANK + n:2 * RANK + n + 1] = jnp.sum(s, axis=0, keepdims=True)
    ls[0, 2 * RANK + 6:] = jnp.zeros((2, SEQ), F32)
    for dx in range(1, NX):
        send(ls.at[0], ls.at[dx], s_st.at[dx], r_st.at[dx], (mod4(x + dx), z, y, c))
    early = es[0]
    for dx in range(1, NX):
        arrived(es.at[dx], r_es.at[dx])
        early = early + es[dx]
    late = ls[0]
    for dx in range(1, NX):
        arrived(ls.at[dx], r_st.at[dx])
        late = late + ls[dx]
    inv = 1.0 / WIDTH
    m1, e_gd, e_g = [early[2 * RANK + n:2 * RANK + n + 1] * inv for n in range(3)]
    mu, e_hh, e_hd, e_gh, e_ghh, e_ghd = [late[2 * RANK + n:2 * RANK + n + 1] * inv for n in range(6)]
    rinv = lax.rsqrt(e_hh - mu * mu + 1e-05)
    m2 = rinv * (e_hd - mu * m1)
    g_n = rinv * (e_gh - mu * e_g)
    g_nn = rinv * rinv * (e_ghh - 2.0 * mu * e_gh + mu * mu * e_g)
    g_nd = rinv * (e_ghd - mu * e_gd)
    lr = live * rinv
    m3 = lr * (e_gd - m1 * e_g - m2 * g_n)
    m4 = lr * (g_nd - m1 * g_n - m2 * g_nn)
    b_one = jnp.broadcast_to(early[RANK:2 * RANK, 0:1], (RANK, SEQ))
    b_g = jnp.broadcast_to(early[RANK:2 * RANK, SEQ - 1:SEQ], (RANK, SEQ))
    b_n = rinv * (late[0:RANK] - mu * b_one)
    b_gn = rinv * (late[RANK:2 * RANK] - mu * b_g)
    b_c = lr * (early[0:RANK] - m1 * b_g - m2 * b_gn)
    q1, q2 = split2(rinv * (b_c - m3 * b_one - m4 * b_n))
    xq = y
    qg[xq] = jnp.concatenate([q1, q2], axis=0).T
    for dy in range(1, NY):
        send(qg.at[xq], qg.at[xq], s_q.at[dy], r_q.at[dy], dev(0, 0, dy))

    z1, z2 = split2(jnp.concatenate([zall[0], zall[1]], axis=0))
    zs = jnp.concatenate([z1, z2], axis=0)
    for cc in range(2):
        rows = pl.ds(cc * HALF, HALF)
        n = (h_ref[rows] - mu) * rinv
        cot = lr * gh_ref[rows] * (dh_ref[rows] - m1 - n * m2)
        g1, g2 = split2(rinv * (cot - m3 - n * m4))
        hb = dot(zs, g1, NT) + dot(zs, g2, NT)
        hb = hb[0:RANK] + hb[RANK:]
        for p in range(NX):
            hb_snd[cc, p] = hb[16 * p:16 * (p + 1)]
    send(hb_snd.at[other], hb_sib, s_hs.at[0], r_hs.at[0], dev(0, 0, 0, 1))
    arrived(hb_sib, r_hs.at[0])
    hb_red[...] = hb_snd[c] + hb_sib[...]
    for dp in range(NX):
        p = mod4(x + dp)
        me = jnp.logical_and(diag, dp == 0)
        send_unless(me, hb_red.at[p], hb_rcv.at[y], s_hb.at[dp], r_hb.at[y], (p, z, x, c))

    @pl.when(diag)
    def _():
        hb_rcv[y] = hb_red[x]

    for dy in range(1, NY):
        arrived(qg.at[xq], r_q.at[dy])
    qs = jnp.concatenate([qg[xb] for xb in range(NX)], axis=0)
    mine = pl.ds(pl.multiple_of(x * 160, 32), 160)
    for cc in range(2):
        t = dot(jnp.concatenate([ctxg[xb, cc, mine] for xb in range(NX)], axis=1), qs)
        ha_snd[cc] = t + pltpu.roll(t, RANK, 1)
    send(ha_snd.at[other], ha_sib, s_ha.at[0], r_ha.at[0], dev(0, 0, 0, 1))
    arrived(ha_sib, r_ha.at[0])
    ha_sum[...] = ha_snd[c] + ha_sib[...]
    low = lax.broadcasted_iota(jnp.int32, (NZ, SEQ), 1) < RANK
    pairs = []
    for k in range(5):
        pairs.append(jnp.where(low, ha_sum[pl.ds(2 * k, NZ, stride=10)], ha_sum[pl.ds(2 * k + 1, NZ, stride=10)]))
    v = jnp.concatenate(pairs, axis=1)
    for zi in range(NZ):
        ha2[zi] = v[zi:zi + 1]
    for dz in range(1, NZ):
        send(ha2.at[lax.rem(z + dz, NZ)], haz.at[dz], s_az.at[dz], r_az.at[dz], dev(0, dz))
    for ys in range(NY):
        @pl.when(jnp.logical_not(jnp.logical_and(diag, y == ys)))
        def _():
            arrived(hb_rcv.at[ys], r_hb.at[ys])
    acc = hb_rcv[0] + hb_rcv[1] + hb_rcv[2] + hb_rcv[3]
    for zi in range(NZ):
        hb2[zi] = acc[zi:zi + 1]
    for dz in range(1, NZ):
        send(hb2.at[lax.rem(z + dz, NZ)], hbz.at[dz], s_bz.at[dz], r_bz.at[dz], dev(0, dz))
    acc = ha2[z]
    for dz in range(1, NZ):
        arrived(haz.at[dz], r_az.at[dz])
        acc = acc + haz[dz]
    for k in range(10):
        out_a[k:k + 1] = acc[:, k * RANK:(k + 1) * RANK]
    acc = hb2[z]
    for dz in range(1, NZ):
        arrived(hbz.at[dz], r_bz.at[dz])
        acc = acc + hbz[dz]
    out_b[...] = acc

    for keep, cp in pending:
        if keep is None:
            cp.wait_send()
        else:
            @pl.when(keep)
            def _():
                cp.wait_send()


def body(ctx, resid, w, a, b, d, u, gain, lengths):
    vmem = pl.BlockSpec(memory_space=pltpu.VMEM)
    dma = lambda *n: pltpu.SemaphoreType.DMA(n)
    return pl.pallas_call(
        kernel,
        out_shape=(jax.ShapeDtypeStruct((10, RANK), F32), jax.ShapeDtypeStruct((1, HALF), F32)),
        in_specs=[pl.BlockSpec(memory_space=pltpu.HBM)] * 9,
        out_specs=(vmem, vmem),
        scratch_shapes=[
            pltpu.VMEM((2 * SEQ, HALF), BF),
            pltpu.VMEM((2 * SEQ, HALF), BF),
            pltpu.VMEM((2 * RANK, HALF), BF),
            pltpu.VMEM((5, SEQ), F32),
            pltpu.SMEM((2,), jnp.int32),
            pltpu.VMEM((2, HALF, SEQ), BF),
            pltpu.VMEM((NX, NC, HALF, SEQ), BF),
            pltpu.VMEM((NC, NZ, COLS, HALF), BF),
            pltpu.VMEM((NC, 2 * RANK, HALF), BF),
            pltpu.VMEM((2, HALF + 16, SEQ), BF),
            pltpu.VMEM((NX, 2, HALF + 16, SEQ), BF),
            pltpu.VMEM((2, HALF + 16, SEQ), BF),
            pltpu.VMEM((NC, HALF, SEQ), BF),
            pltpu.VMEM((NC, 8, SEQ), F32),
            pltpu.VMEM((NX, FEATS, SEQ), BF),
            pltpu.VMEM((NY, FEATS, SEQ), BF),
            pltpu.VMEM((SEQ, SEQ), F32),
            pltpu.VMEM((NY, 32, SEQ), F32),
            pltpu.VMEM((32, SEQ), F32),
            pltpu.VMEM((NY, 32, SEQ), F32),
            pltpu.VMEM((NX, 2 * RANK + 8, SEQ), F32),
            pltpu.VMEM((NX, 2 * RANK + 8, SEQ), F32),
            pltpu.VMEM((FEATS, SEQ), F32),
            pltpu.VMEM((FEATS, SEQ), F32),
            pltpu.VMEM((FEATS, SEQ), F32),
            pltpu.VMEM((NX, SEQ, SEQ), BF),
            pltpu.VMEM((NC, 160, SEQ), F32),
            pltpu.VMEM((160, SEQ), F32),
            pltpu.VMEM((NC, NX, 16, HALF), F32),
            pltpu.VMEM((NX, 16, HALF), F32),
            pltpu.VMEM((NX, 16, HALF), F32),
            pltpu.VMEM((NY, 16, HALF), F32),
            pltpu.VMEM((160, SEQ), F32),
            pltpu.VMEM((NZ, 1, HALF), F32),
            pltpu.VMEM((NZ, 1, HALF), F32),
            pltpu.VMEM((NZ, 1, HALF), F32),
            pltpu.VMEM((NZ, 1, HALF), F32),
            dma(9),
            dma(7), dma(7), dma(16 * NP), dma(16 * NP), dma(16), dma(16), dma(1), dma(1), dma(2), dma(NX, 2), dma(NX, 2), dma(2),
            dma(8), dma(4), dma(NX, NCH), dma(NY, NCH),
            dma(NY), dma(NY), dma(NX), dma(NY), dma(NX), dma(NX), dma(NX), dma(NX), dma(NY), dma(NY), dma(1), dma(1),
            dma(1), dma(1),
            dma(NX), dma(NY), dma(NZ), dma(NZ), dma(NZ), dma(NZ),
        ],
        compiler_params=pltpu.CompilerParams(collective_id=0, has_side_effects=True, vmem_limit_bytes=60 << 20),
        cost_estimate=pl.CostEstimate(flops=2 * 1280 * 1280 * 512, bytes_accessed=2 << 20, transcendentals=0),
        name="hvp",
    )(ctx, resid, w.T, a.T, d.T, b, u, gain.reshape(5, SEQ), lengths)


def solution(mesh):
    grid = Mesh(mesh.devices.reshape(NX, NZ, NY, NC), AXES)
    dp, tensor = ("x", "z"), ("y", "c")
    in_specs = (
        P(dp, tensor),
        P(dp, tensor),
        P(tensor, dp),
        P(tensor, None),
        P(None, tensor),
        P(tensor, None),
        P(None, tensor),
        P(tensor),
        P(dp),
    )
    out_specs = (P(("y", "c", "x", "z"), None), P(dp, tensor))
    return jax.shard_map(body, mesh=grid, in_specs=in_specs, out_specs=out_specs, check_vma=False)
```

```python
import functools

import jax
import jax.numpy as jnp
from jax import lax
from jax.experimental import pallas as pl
from jax.experimental.pallas import tpu as pltpu
from jax.sharding import Mesh, PartitionSpec as P

AXES = ("x", "z", "y", "c")
NX, NZ, NY, NC = 4, 16, 4, 2
SEQ = 128
RANK = 64
FEATS = 1280
HALF = 640
COLS = 80
TOKENS = 16384
WIDTH = 5120
BF = jnp.bfloat16
F32 = jnp.float32
CHUNKS = ((0, 1),) + tuple((2 * s - 1, 2 * s + 1) for s in range(1, 7)) + ((13, 16),)
PARTS = tuple((16 * i, 16) for i in range(5))
NP = len(PARTS)
NCH = len(CHUNKS)
NT = (((1,), (1,)), ((), ()))
TN = (((0,), (0,)), ((), ()))


def split2(v):
    hi = v.astype(BF)
    lo = (v - hi.astype(F32)).astype(BF)
    return hi, lo


def split3(v):
    hi = v.astype(BF)
    rest = v - hi.astype(F32)
    mid = rest.astype(BF)
    lo = (rest - mid.astype(F32)).astype(BF)
    return hi, mid, lo


def dot(a, b, dims=(((1,), (0,)), ((), ()))):
    return lax.dot_general(a, b, dims, preferred_element_type=F32)


def kernel(
    ctx_ref, resid_ref, wt_ref, at_ref, dt_ref, b_ref, u_ref, g_ref, len_ref,
    out_a, out_b,
    ctx_v, resid_v, bu_v, g_v, len_v,
    ctxs, ctxg, wg, adg, rt, relay, rrecv, buT, gr, part, rsb, zp, zr, zsum, zall, es, ts, ls, h_ref, dh_ref, gh_ref,
    qg, ha_snd, ha_sib, hb_snd, hb_sib, hb_red, hb_rcv, ha_sum, ab, abz,
    s_in, s_ctx, r_ctx, s_w, r_w, s_ws, r_ws, s_ad, r_ad, s_res, r_res, s_rel, r_rel, s_bu, r_bu, s_rs, r_rs,
    s_zr, r_zr, s_zd, r_zd, s_es, r_es, s_ts, r_ts, s_st, r_st, s_q, r_q, s_ha, r_ha, s_hs, r_hs, s_hb, r_hb, s_ab, r_ab,
):
    x, z, y, c = [lax.axis_index(a) for a in AXES]
    other = lax.rem(c + 1, NC)
    diag = x == y

    def mod4(v):
        return lax.rem(v + 8, 4)

    def dev(dx=0, dz=0, dy=0, dc=0):
        return (mod4(x + dx), lax.rem(z + dz + NZ, NZ), mod4(y + dy), lax.rem(c + dc, NC))

    def rcopy(src, dst, ss, rs, to):
        return pltpu.make_async_remote_copy(
            src_ref=src, dst_ref=dst, send_sem=ss, recv_sem=rs, device_id=to, device_id_type=pl.DeviceIdType.MESH
        )

    def arrived(dst, rs):
        rcopy(dst, dst, s_ad.at[0], rs, dev(0, 0, 0, 1)).wait_recv()

    def left(src, ss):
        rcopy(src, src, ss, r_ad.at[0], dev(0, 0, 0, 1)).wait_send()

    def send(src, dst, ss, rs, to):
        rcopy(src, dst, ss, rs, to).start()

    def send_unless(cond, src, dst, ss, rs, to):
        @pl.when(jnp.logical_not(cond))
        def _():
            send(src, dst, ss, rs, to)

    def first_three(ref):
        return ref.at[pl.ds(0, 3)]

    def last_three(ref):
        return ref.at[pl.ds(1, 3)]

    loads = [
        pltpu.make_async_copy(src, dst, s_in.at[i])
        for i, (src, dst) in enumerate((
            (wt_ref, wg.at[c, 0]),
            (ctx_ref, ctx_v),
            (at_ref, adg.at[c, pl.ds(0, RANK)]),
            (dt_ref, adg.at[c, pl.ds(RANK, RANK)]),
            (resid_ref, resid_v),
            (b_ref, bu_v.at[pl.ds(0, RANK)]),
            (u_ref, bu_v.at[pl.ds(RANK, RANK)]),
            (g_ref, g_v),
            (len_ref, len_v),
        ))
    ]
    for cp in loads:
        cp.start()

    barrier = pltpu.get_barrier_semaphore()
    first_partners = [dev(0, dz) for dz in (-1, 1)]
    first_partners += [dev(dx, 0, 0, dc) for dx in (1, 3, 2) for dc in range(NC)]
    first_partners += [dev(0, 0, dy, dc) for dy in (1, 3, 2) for dc in range(NC)]
    first_partners += [dev(0, 0, 0, 1)]
    for partner in first_partners:
        pl.semaphore_signal(barrier, inc=1, device_id=partner, device_id_type=pl.DeviceIdType.MESH)
    count = len(first_partners)
    pl.semaphore_wait(barrier, count)

    def w_copy(s, flow, sub):
        if s == 8:
            src, dst = 11 + flow, 15
        else:
            src, dst = (0 if s == 1 else 2 * s - 3 + flow), 2 * s - 1 + flow
        rows = pl.ds(*PARTS[sub])
        source = wt_ref.at[rows] if s == 1 else wg.at[c, src, rows]
        return rcopy(source, wg.at[c, dst, rows], s_w.at[0], r_w.at[NP * (s - 1) + sub], dev(0, (1 - 2 * flow) * (2 if s == 8 else 1)))

    def w_start(s, flow, sub):
        w_copy(s, flow, sub).start()

    def w_sib(slot):
        k = min((slot + 1) // 2, 7)
        send(wg.at[c, slot], wg.at[c, slot], s_ws.at[0], r_ws.at[k], dev(0, 0, 0, 1))

    def first(sub):
        for flow in range(2):
            w_start(1, flow, sub)

    first(0)
    loads[1].wait()
    for half in range(2):
        ctxs[half] = ctx_v[half * SEQ:(half + 1) * SEQ, :].T
    lead = 1 - 2 * c
    ctx_sends_to = lambda dx, k: [
        send(ctxs.at[half], ctxg.at[x, c], s_ctx.at[0], r_ctx.at[k], (mod4(x + dx), z, y, half))
        for half in range(2)
    ]
    ctx_sends_to(lead, jnp.where(c == 0, 1, 4))
    send(ctxs.at[other], ctxg.at[x, c], s_ctx.at[1], r_ctx.at[0], dev(0, 0, 0, 1))
    loads[0].wait()
    w_sib(0)
    loads[2].wait()
    loads[3].wait()
    send(adg.at[c], adg.at[c], s_ad.at[0], r_ad.at[0], dev(0, 0, 0, 1))
    ctxg[x, c] = ctxs[c]

    loads[4].wait()
    loads[8].wait()
    lane = lax.broadcasted_iota(jnp.int32, (16, SEQ), 1)
    off = jnp.logical_not(diag)
    for half in range(2):
        rt[half, 0:HALF] = resid_v[half * SEQ:(half + 1) * SEQ, :].T
        rt[half, HALF:] = jnp.where(lane < len_v[half], 1.0, 0.0).astype(BF)

        @pl.when(jnp.logical_and(diag, c == half))
        def _():
            rrecv[c] = rt[half]

    send_unless(diag, rt.at[0], relay.at[y, c], s_res.at[0], r_res.at[0], (x, z, x, 0))
    send_unless(jnp.logical_or(off, c == 0), rt.at[0], rrecv.at[c], s_res.at[0], r_rel.at[c], (x, z, x, 0))
    first(1)
    first(2)
    for i in (5, 6, 7):
        loads[i].wait()

    @pl.when(diag)
    def _():
        buT[c] = bu_v[...].T
        gr[c] = jnp.concatenate([g_v[...], jnp.zeros((3, SEQ), F32)], axis=0)

    for dy in range(1, NY):
        send_unless(off, buT.at[c], buT.at[c], s_bu.at[0], r_bu.at[0], dev(0, 0, dy))
        send_unless(off, gr.at[c], gr.at[c], s_bu.at[1], r_bu.at[1], dev(0, 0, dy))

    first(3)
    first(4)
    def block(j):
        return mod4(x + j)

    def mm(js, k):
        lo, hi = CHUNKS[k]
        rows = (hi - lo) * COLS
        rhs = [jnp.concatenate([ctxg[block(j), cc] for j in js], axis=1) for cc in range(2)]
        lhs = [wg[cc, lo:hi].reshape(rows, HALF) for cc in range(2)]
        out = (dot(lhs[0], rhs[0]) + dot(lhs[1], rhs[1])).astype(BF)
        piece = pl.ds(lo * COLS, rows)
        for i, j in enumerate(js):
            part[j, piece] = out[:, i * SEQ:(i + 1) * SEQ]
            dest = mod4(x + j)
            send_unless(
                dest == y, part.at[j, piece], rsb.at[y, piece], s_rs.at[0], r_rs.at[k // (NCH - 1)], (x, z, dest, c)
            )

    def last_hop(flow):
        return (0, 2, 4) if flow == 0 else (1, 3)

    def w_take(s, sub):
        rows = pl.ds(*PARTS[sub])
        arrived(wg.at[0, 0, rows] if s == 8 else wg.at[pl.ds(0, 2), 0, rows], r_w.at[NP * (s - 1) + sub])
        for flow in range(2):
            if s < 7:
                w_start(s + 1, flow, sub)
            if s == 6 and sub in last_hop(flow):
                w_start(8, flow, sub)
        if sub == NP - 1:
            for slot in range(2 * s - 1, min(2 * s + 1, NZ)):
                w_sib(slot)

    def sib_wait(k):
        lo, hi = CHUNKS[k]
        arrived(wg.at[c, pl.ds(lo, hi - lo)], r_ws.at[k])

    def ctx_forward(i, dx_src, half_c, to_dx):
        blk = ctxg.at[mod4(x + dx_src), half_c]
        send(blk, blk, s_ctx.at[0], r_ctx.at[i], dev(to_dx))

    def ctx_wait(i):
        arrived(ctxg.at[0, 0], r_ctx.at[i])

    def low_rank_sum():
        acc = zp[pl.ds(pl.multiple_of(y * 32, 32), 32)]
        arrived(last_three(zr), r_zr.at[0])
        for dy in range(1, NY):
            acc = acc + zr[dy]
        zsum[...] = acc
        for dq in range(NX):
            me = jnp.logical_and(diag, dq == 0)
            send_unless(me, zsum, zall.at[y], s_zd.at[0], r_zd.at[0], (mod4(x + dq), z, x, c))

        @pl.when(diag)
        def _():
            zall[y] = acc

    def resid_half():
        send_unless(jnp.logical_and(diag, c == 1), rt.at[1], rrecv.at[c], s_res.at[1], r_rel.at[c], (y, z, x, 1))

    def second_leg():
        pass_on = jnp.logical_and(diag, c == 0)

        @pl.when(pass_on)
        def _():
            arrived(first_three(relay), r_res.at[0])

        for dq in range(1, NX):
            q = mod4(x + dq)
            for cc in range(2):
                send_unless(
                    jnp.logical_not(pass_on), relay.at[q, cc], rrecv.at[cc], s_rel.at[0], r_rel.at[cc], (q, z, x, 0)
                )

    def adapter_on():
        @pl.when(off)
        def _():
            arrived(buT.at[c], r_bu.at[0])
            arrived(gr.at[c], r_bu.at[1])

        send(buT.at[c], buT.at[c], s_bu.at[2], r_bu.at[2], dev(0, 0, 0, 1))
        send(gr.at[c], gr.at[c], s_bu.at[3], r_bu.at[3], dev(0, 0, 0, 1))

    def hop(s, *work):
        for sub in range(NP):
            w_take(s, sub)
            for f in work[len(work) * sub // NP:len(work) * (sub + 1) // NP]:
                f()

    def zp_sum():
        ctx_wait(0)
        arrived(adg.at[c], r_ad.at[0])
        zp[...] = dot(adg[0], ctxg[x, 0]) + dot(adg[1], ctxg[x, 1])

    def zp_send():
        for dy in range(1, NY):
            rows = pl.ds(pl.multiple_of(mod4(y + dy) * 32, 32), 32)
            send(zp.at[rows], zr.at[dy], s_zr.at[0], r_zr.at[0], dev(0, 0, dy))

    def ctx_near():
        ctx_wait(2)
        ctx_wait(3)

    def ctx_pass():
        ctx_wait(1)
        ctx_forward(5, -1, 0, 1)
        ctx_wait(4)
        ctx_forward(6, 1, 1, -1)

    def ctx_far():
        ctx_wait(5)
        ctx_wait(6)

    def m(js, *ks):
        return lambda: [mm(js, k) for k in ks]

    def sw(k):
        return lambda: sib_wait(k)

    ctx_second = lambda: ctx_sends_to(-lead, jnp.where(c == 0, 3, 2))

    def low_rank_terms():
        @pl.when(diag)
        def _():
            arrived(first_three(zall), r_zd.at[0])

        @pl.when(off)
        def _():
            arrived(zall, r_zd.at[0])

        arrived(buT.at[c], r_bu.at[2])
        arrived(gr.at[c], r_bu.at[3])
        zt = jnp.concatenate([zall[0], zall[1]], axis=0)
        ztt = jnp.concatenate([zall[2], zall[3]], axis=0)
        zero = jnp.zeros((RANK, SEQ), F32)
        rhs = jnp.concatenate([jnp.concatenate([ztt, zt], axis=0), jnp.concatenate([zt, zero], axis=0)], axis=1)
        r1, r2, r3 = split3(rhs)
        for cc in range(2):
            b = buT[cc]
            both = dot(b, r1) + dot(b, r2) + dot(b, r3)
            dh_ref[cc * HALF:(cc + 1) * HALF] = both[:, 0:SEQ]
            h_ref[cc * HALF:(cc + 1) * HALF] = both[:, SEQ:]

    def fold(v):
        return jnp.sum(v.reshape(-1, 8, SEQ), axis=0)

    def early_sums():
        for i in range(10):
            col = jnp.broadcast_to(gr[i // 5, pl.ds(i % 5, 1)], (SEQ, SEQ)).T
            gh_ref[i * SEQ:(i + 1) * SEQ] = col * col
        acc = jnp.zeros((SEQ, 3 * SEQ), F32)
        sums = [jnp.zeros((8, SEQ), F32) for _ in range(3)]
        lane = lax.broadcasted_iota(jnp.int32, (HALF, SEQ), 1)
        for cc in range(2):
            rows = pl.ds(cc * HALF, HALF)
            g2 = gh_ref[rows]
            d = dh_ref[rows]
            gd = g2 * d
            d1, d2 = split2(gd)
            k1, k2 = split2(jnp.where(lane < RANK, 1.0, g2))
            acc = acc + dot(buT[cc], jnp.concatenate([d1, d2, k1], axis=1), TN)
            e2 = dot(buT[cc], k2, TN)
            acc = acc + jnp.concatenate([jnp.zeros((SEQ, 2 * SEQ), F32), e2], axis=1)
            sums = [s + fold(t) for s, t in zip(sums, (d, gd, g2))]
        es[0, 0:RANK] = acc[0:RANK, 0:SEQ] + acc[0:RANK, SEQ:2 * SEQ]
        es[0, RANK:2 * RANK] = acc[0:RANK, 2 * SEQ:]
        for n, s in enumerate(sums):
            es[0, 2 * RANK + n:2 * RANK + n + 1] = jnp.sum(s, axis=0, keepdims=True)
        es[0, 2 * RANK + 3:] = jnp.zeros((5, SEQ), F32)

    def early_send():
        for dx in range(1, NX):
            send(es.at[0], es.at[dx], s_es.at[0], r_es.at[0], (mod4(x + dx), z, y, c))

    both = lambda *fs: lambda: [f() for f in fs]
    idle = lambda: None

    hop(1, ctx_second, zp_sum, zp_send)
    hop(2, sw(0), m((0,), 0), ctx_pass)
    hop(3, both(sw(1), m((0,), 1)), idle, ctx_near)
    hop(4, both(sw(2), m((0,), 2), m((1, 3), 0)), both(m((1, 3), 1, 2)), both(low_rank_sum, resid_half, adapter_on))
    hop(5, both(sw(3), m((0,), 3)), both(m((1, 3), 3), ctx_far), m((2,), 0, 1))
    hop(6, both(sw(4), m((1, 3), 4)), both(m((0, 2), 4), second_leg), m((2,), 2, 3))
    hop(7, both(sw(5), m((1, 3), 5)), m((0, 2), 5), low_rank_terms)
    hop(8, sw(6), m((1, 3), 6), m((0, 2), 6))
    sib_wait(7)
    mm((1, 3), 7)
    mm((2, 0), 7)
    early_sums()
    early_send()

    for cc in range(2):
        @pl.when(jnp.logical_not(jnp.logical_and(diag, c == cc)))
        def _():
            arrived(rrecv.at[cc], r_rel.at[cc])
        h_ref[cc * HALF:(cc + 1) * HALF] = h_ref[cc * HALF:(cc + 1) * HALF] + rrecv[cc, 0:HALF].astype(F32)
    live = rrecv[0, HALF:].astype(F32)[0:1] * (1.0 / jnp.sqrt(jnp.float32(TOKENS)))

    jown = mod4(y - x)
    for k, (lo, hi) in enumerate(CHUNKS):
        if k in (0, NCH - 1):
            start = lo * COLS
            rows = pl.ds(start, (CHUNKS[-2][1] if k == 0 else hi) * COLS - start)
            arrived(rsb.at[pl.ds(0, 3), rows], r_rs.at[k // (NCH - 1)])
        for slot in range(lo, hi):
            step = (slot + 1) // 2
            zz = z if slot == 0 else (z - step if slot % 2 == 1 else z + step)
            zz = lax.rem(zz + NZ, NZ)
            rows = pl.ds(pl.multiple_of(zz * COLS, 16), COLS)
            piece = pl.ds(slot * COLS, COLS)
            acc = part[jown, piece].astype(F32)
            for dy in range(1, NY):
                acc = acc + rsb[mod4(y - dy), piece].astype(F32)
            h_ref[rows] = h_ref[rows] + acc

    acc = jnp.zeros((SEQ, 4 * SEQ), F32)
    sums = [jnp.zeros((8, SEQ), F32) for _ in range(6)]
    for cc in range(2):
        rows = pl.ds(cc * HALF, HALF)
        h = h_ref[rows]
        d = dh_ref[rows]
        g2 = gh_ref[rows]
        gh = g2 * h
        h1, h2 = split2(h)
        g1, g3 = split2(gh)
        acc = acc + dot(buT[cc], jnp.concatenate([h1, h2, g1, g3], axis=1), TN)
        sums = [s + fold(t) for s, t in zip(sums, (h, h * h, h * d, gh, gh * h, gh * d))]
    for n, s in enumerate(sums):
        ts[0, n:n + 1] = jnp.sum(s, axis=0, keepdims=True)
    ts[0, 6:] = jnp.zeros((2, SEQ), F32)
    for dx in (2, 1, 3):
        send(ts.at[0], ts.at[dx], s_ts.at[0], r_ts.at[0], (mod4(x + dx), z, y, c))
    ls[0, 0:RANK] = acc[0:RANK, 0:SEQ] + acc[0:RANK, SEQ:2 * SEQ]
    ls[0, RANK:] = acc[0:RANK, 2 * SEQ:3 * SEQ] + acc[0:RANK, 3 * SEQ:]
    for dx in (2, 1, 3):
        send(ls.at[0], ls.at[dx], s_st.at[0], r_st.at[0], (mod4(x + dx), z, y, c))
    early = es[0]
    arrived(last_three(es), r_es.at[0])
    for dx in range(1, NX):
        early = early + es[dx]
    late = ts[0]
    arrived(last_three(ts), r_ts.at[0])
    for dx in range(1, NX):
        late = late + ts[dx]
    inv = 1.0 / WIDTH
    m1, e_gd, e_g = [early[2 * RANK + n:2 * RANK + n + 1] * inv for n in range(3)]
    mu, e_hh, e_hd, e_gh, e_ghh, e_ghd = [late[n:n + 1] * inv for n in range(6)]
    rinv = lax.rsqrt(e_hh - mu * mu + 1e-05)
    m2 = rinv * (e_hd - mu * m1)
    g_n = rinv * (e_gh - mu * e_g)
    g_nn = rinv * rinv * (e_ghh - 2.0 * mu * e_gh + mu * mu * e_g)
    g_nd = rinv * (e_ghd - mu * e_gd)
    lr = live * rinv
    m3 = lr * (e_gd - m1 * e_g - m2 * g_n)
    m4 = lr * (g_nd - m1 * g_n - m2 * g_nn)
    late = ls[0]
    arrived(last_three(ls), r_st.at[0])
    for dx in range(1, NX):
        late = late + ls[dx]
    b_one = jnp.broadcast_to(early[RANK:2 * RANK, 0:1], (RANK, SEQ))
    b_g = jnp.broadcast_to(early[RANK:2 * RANK, SEQ - 1:SEQ], (RANK, SEQ))
    b_n = rinv * (late[0:RANK] - mu * b_one)
    b_gn = rinv * (late[RANK:2 * RANK] - mu * b_g)
    b_c = lr * (early[0:RANK] - m1 * b_g - m2 * b_gn)
    q1, q2 = split2(rinv * (b_c - m3 * b_one - m4 * b_n))
    xq = y
    qg[xq] = jnp.concatenate([q1, q2], axis=0).T
    for dy in (2, 1, 3):
        send(qg.at[xq], qg.at[xq], s_q.at[0], r_q.at[0], dev(0, 0, dy))

    z1, z2 = split2(jnp.concatenate([zall[0], zall[1]], axis=0))
    zs = jnp.concatenate([z1, z2], axis=0)
    for cc in range(2):
        rows = pl.ds(cc * HALF, HALF)
        n = (h_ref[rows] - mu) * rinv
        cot = lr * gh_ref[rows] * (dh_ref[rows] - m1 - n * m2)
        g1, g2 = split2(rinv * (cot - m3 - n * m4))
        hb = dot(zs, g1, NT) + dot(zs, g2, NT)
        hb = hb[0:RANK] + hb[RANK:]
        for p in range(NX):
            hb_snd[cc, p] = hb[16 * p:16 * (p + 1)]
    send(hb_snd.at[other], hb_sib, s_hs.at[0], r_hs.at[0], dev(0, 0, 0, 1))
    arrived(hb_sib, r_hs.at[0])
    hb_red[...] = hb_snd[c] + hb_sib[...]
    for dp in range(NX):
        p = mod4(x + dp)
        me = jnp.logical_and(diag, dp == 0)
        send_unless(me, hb_red.at[p], hb_rcv.at[y], s_hb.at[0], r_hb.at[0], (p, z, x, c))

    @pl.when(diag)
    def _():
        hb_rcv[y] = hb_red[x]

    arrived(first_three(qg), r_q.at[0])
    qs = jnp.concatenate([qg[xb] for xb in range(NX)], axis=0)
    mine = pl.ds(pl.multiple_of(x * 160, 32), 160)
    for cc in range(2):
        t = dot(jnp.concatenate([ctxg[xb, cc, mine] for xb in range(NX)], axis=1), qs)
        ha_snd[cc] = t + pltpu.roll(t, RANK, 1)
    send(ha_snd.at[other], ha_sib, s_ha.at[0], r_ha.at[0], dev(0, 0, 0, 1))
    arrived(ha_sib, r_ha.at[0])
    ha_sum[...] = ha_snd[c] + ha_sib[...]
    low = lax.broadcasted_iota(jnp.int32, (NZ, SEQ), 1) < RANK
    pairs = []
    for k in range(5):
        pairs.append(jnp.where(low, ha_sum[pl.ds(2 * k, NZ, stride=10)], ha_sum[pl.ds(2 * k + 1, NZ, stride=10)]))
    v = jnp.concatenate(pairs, axis=1)
    @pl.when(diag)
    def _():
        arrived(first_three(hb_rcv), r_hb.at[0])

    @pl.when(off)
    def _():
        arrived(hb_rcv, r_hb.at[0])

    v = jnp.concatenate([v, hb_rcv[0] + hb_rcv[1] + hb_rcv[2] + hb_rcv[3]], axis=1)
    for zi in range(NZ):
        ab[zi] = v[zi:zi + 1]
    for dz in (8, 7, 9, 6, 10, 5, 11, 4, 12, 3, 13, 2, 14, 1, 15):
        send(ab.at[lax.rem(z + dz, NZ)], abz.at[dz], s_ab.at[0], r_ab.at[0], dev(0, dz))
    acc = ab[z]
    arrived(abz.at[pl.ds(1, NZ - 1)], r_ab.at[0])
    for dz in range(1, NZ):
        acc = acc + abz[dz]
    for k in range(10):
        out_a[k:k + 1] = acc[:, k * RANK:(k + 1) * RANK]
    out_b[...] = acc[:, HALF:]

    left(wg.at[c, pl.ds(0, NZ - 1)], s_w.at[0])
    left(wg.at[c], s_ws.at[0])
    left(first_three(ctxg), s_ctx.at[0])
    left(ctxg.at[0, 0], s_ctx.at[1])
    left(adg.at[c], s_ad.at[0])
    for half in range(2):
        @pl.when(jnp.logical_not(jnp.logical_and(diag, c == half)))
        def _():
            left(rt.at[half], s_res.at[half])

    @pl.when(jnp.logical_and(diag, c == 0))
    def _():
        left(first_three(relay), s_rel.at[0])

    left(buT.at[c], s_bu.at[2])
    left(gr.at[c], s_bu.at[3])
    left(first_three(part), s_rs.at[0])
    left(first_three(zr), s_zr.at[0])
    left(first_three(es), s_es.at[0])
    left(first_three(ts), s_ts.at[0])
    left(first_three(ls), s_st.at[0])
    left(first_three(qg), s_q.at[0])
    left(hb_sib, s_hs.at[0])
    left(ha_sib, s_ha.at[0])
    left(ab.at[pl.ds(0, NZ - 1)], s_ab.at[0])

    @pl.when(diag)
    def _():
        left(ctxg.at[pl.ds(0, 3), 0], s_bu.at[0])
        left(first_three(ts), s_bu.at[1])
        left(first_three(zall), s_zd.at[0])
        left(first_three(hb_red), s_hb.at[0])

    @pl.when(off)
    def _():
        left(zall, s_zd.at[0])
        left(hb_red, s_hb.at[0])


def body(ctx, resid, w, a, b, d, u, gain, lengths):
    vmem = pl.BlockSpec(memory_space=pltpu.VMEM)
    dma = lambda *n: pltpu.SemaphoreType.DMA(n)
    return pl.pallas_call(
        kernel,
        out_shape=(jax.ShapeDtypeStruct((10, RANK), F32), jax.ShapeDtypeStruct((1, HALF), F32)),
        in_specs=[pl.BlockSpec(memory_space=pltpu.HBM)] * 9,
        out_specs=(vmem, vmem),
        scratch_shapes=[
            pltpu.VMEM((2 * SEQ, HALF), BF),
            pltpu.VMEM((2 * SEQ, HALF), BF),
            pltpu.VMEM((2 * RANK, HALF), BF),
            pltpu.VMEM((5, SEQ), F32),
            pltpu.SMEM((2,), jnp.int32),
            pltpu.VMEM((2, HALF, SEQ), BF),
            pltpu.VMEM((NX, NC, HALF, SEQ), BF),
            pltpu.VMEM((NC, NZ, COLS, HALF), BF),
            pltpu.VMEM((NC, 2 * RANK, HALF), BF),
            pltpu.VMEM((2, HALF + 16, SEQ), BF),
            pltpu.VMEM((NX, 2, HALF + 16, SEQ), BF),
            pltpu.VMEM((2, HALF + 16, SEQ), BF),
            pltpu.VMEM((NC, HALF, SEQ), BF),
            pltpu.VMEM((NC, 8, SEQ), F32),
            pltpu.VMEM((NX, FEATS, SEQ), BF),
            pltpu.VMEM((NY, FEATS, SEQ), BF),
            pltpu.VMEM((SEQ, SEQ), F32),
            pltpu.VMEM((NY, 32, SEQ), F32),
            pltpu.VMEM((32, SEQ), F32),
            pltpu.VMEM((NY, 32, SEQ), F32),
            pltpu.VMEM((NX, 2 * RANK + 8, SEQ), F32),
            pltpu.VMEM((NX, 8, SEQ), F32),
            pltpu.VMEM((NX, 2 * RANK, SEQ), F32),
            pltpu.VMEM((FEATS, SEQ), F32),
            pltpu.VMEM((FEATS, SEQ), F32),
            pltpu.VMEM((FEATS, SEQ), F32),
            pltpu.VMEM((NX, SEQ, SEQ), BF),
            pltpu.VMEM((NC, 160, SEQ), F32),
            pltpu.VMEM((160, SEQ), F32),
            pltpu.VMEM((NC, NX, 16, HALF), F32),
            pltpu.VMEM((NX, 16, HALF), F32),
            pltpu.VMEM((NX, 16, HALF), F32),
            pltpu.VMEM((NY, 16, HALF), F32),
            pltpu.VMEM((160, SEQ), F32),
            pltpu.VMEM((NZ, 1, 2 * HALF), F32),
            pltpu.VMEM((NZ, 1, 2 * HALF), F32),
            dma(9), dma(2), dma(7), dma(1), dma(8 * NP), dma(1), dma(NCH), dma(1), dma(1), dma(2), dma(1), dma(1), dma(2),
            dma(4), dma(4), dma(1), dma(2),
            dma(1), dma(1), dma(1), dma(1), dma(1), dma(1), dma(1), dma(1), dma(1), dma(1), dma(1), dma(1),
            dma(1), dma(1), dma(1), dma(1), dma(1), dma(1), dma(1), dma(1),
        ],
        compiler_params=pltpu.CompilerParams(collective_id=0, has_side_effects=True, vmem_limit_bytes=60 << 20),
        cost_estimate=pl.CostEstimate(flops=2 * 1280 * 1280 * 512, bytes_accessed=2 << 20, transcendentals=0),
        name="hvp",
    )(ctx, resid, w.T, a.T, d.T, b, u, gain.reshape(5, SEQ), lengths)


def solution(mesh):
    grid = Mesh(mesh.devices.reshape(NX, NZ, NY, NC), AXES)
    dp, tensor = ("x", "z"), ("y", "c")
    in_specs = (
        P(dp, tensor),
        P(dp, tensor),
        P(tensor, dp),
        P(tensor, None),
        P(None, tensor),
        P(tensor, None),
        P(None, tensor),
        P(tensor),
        P(dp),
    )
    out_specs = (P(("y", "c", "x", "z"), None), P(dp, tensor))
    return jax.shard_map(body, mesh=grid, in_specs=in_specs, out_specs=out_specs, check_vma=False)
```

```python
import functools

import jax
import jax.numpy as jnp
from jax import lax
from jax.experimental import pallas as pl
from jax.experimental.pallas import tpu as pltpu
from jax.sharding import Mesh, PartitionSpec as P

AXES = ("x", "z", "y", "c")
NX, NZ, NY, NC = 4, 16, 4, 2
SEQ = 128
RANK = 64
FEATS = 1280
HALF = 640
COLS = 80
TOKENS = 16384
WIDTH = 5120
BF = jnp.bfloat16
F32 = jnp.float32
CHUNKS = ((0, 1),) + tuple((2 * s - 1, 2 * s + 1) for s in range(1, 7)) + ((13, 16),)
PARTS = tuple((16 * i, 16) for i in range(5))
NP = len(PARTS)
NCH = len(CHUNKS)
NT = (((1,), (1,)), ((), ()))
TN = (((0,), (0,)), ((), ()))


def split2(v):
    hi = v.astype(BF)
    lo = (v - hi.astype(F32)).astype(BF)
    return hi, lo


def split3(v):
    hi = v.astype(BF)
    rest = v - hi.astype(F32)
    mid = rest.astype(BF)
    lo = (rest - mid.astype(F32)).astype(BF)
    return hi, mid, lo


def dot(a, b, dims=(((1,), (0,)), ((), ()))):
    return lax.dot_general(a, b, dims, preferred_element_type=F32)


def kernel(
    ctx_ref, resid_ref, wt_ref, at_ref, dt_ref, b_ref, u_ref, g_ref, len_ref,
    out_a, out_b,
    ctx_v, resid_v, bu_v, g_v, len_v,
    ctxs, ctxg, wg, adg, rt, relay, rrecv, buT, gr, part, rsb, zp, zr, zsum, zall, es, ts, ls, h_ref, dh_ref, gh_ref,
    qg, ha_snd, ha_sib, hb_snd, hb_sib, hb_red, hb_rcv, ha_sum, ab, abz,
    s_in, s_ctx, r_ctx, s_w, r_w, s_ws, r_ws, s_ad, r_ad, s_res, r_res, s_rel, r_rel, s_bu, r_bu, s_rs, r_rs,
    s_zr, r_zr, s_zd, r_zd, s_es, r_es, s_ts, r_ts, s_st, r_st, s_q, r_q, s_ha, r_ha, s_hs, r_hs, s_hb, r_hb, s_ab, r_ab,
):
    x, z, y, c = [lax.axis_index(a) for a in AXES]
    other = lax.rem(c + 1, NC)
    diag = x == y

    def mod4(v):
        return lax.rem(v + 8, 4)

    def dev(dx=0, dz=0, dy=0, dc=0):
        return (mod4(x + dx), lax.rem(z + dz + NZ, NZ), mod4(y + dy), lax.rem(c + dc, NC))

    def rcopy(src, dst, ss, rs, to):
        return pltpu.make_async_remote_copy(
            src_ref=src, dst_ref=dst, send_sem=ss, recv_sem=rs, device_id=to, device_id_type=pl.DeviceIdType.MESH
        )

    def arrived(dst, rs):
        rcopy(dst, dst, s_ad.at[0], rs, dev(0, 0, 0, 1)).wait_recv()

    def left(src, ss):
        rcopy(src, src, ss, r_ad.at[0], dev(0, 0, 0, 1)).wait_send()

    def send(src, dst, ss, rs, to):
        rcopy(src, dst, ss, rs, to).start()

    def send_unless(cond, src, dst, ss, rs, to):
        @pl.when(jnp.logical_not(cond))
        def _():
            send(src, dst, ss, rs, to)

    def first_three(ref):
        return ref.at[pl.ds(0, 3)]

    def last_three(ref):
        return ref.at[pl.ds(1, 3)]

    loads = [
        pltpu.make_async_copy(src, dst, s_in.at[i])
        for i, (src, dst) in enumerate((
            (wt_ref, wg.at[c, 0]),
            (ctx_ref, ctx_v),
            (at_ref, adg.at[c, pl.ds(0, RANK)]),
            (dt_ref, adg.at[c, pl.ds(RANK, RANK)]),
            (resid_ref, resid_v),
            (b_ref, bu_v.at[pl.ds(0, RANK)]),
            (u_ref, bu_v.at[pl.ds(RANK, RANK)]),
            (g_ref, g_v),
            (len_ref, len_v),
        ))
    ]
    for cp in loads:
        cp.start()

    barrier = pltpu.get_barrier_semaphore()
    first_partners = [dev(0, dz) for dz in (-1, 1)]
    first_partners += [dev(dx, 0, 0, dc) for dx in (1, 3, 2) for dc in range(NC)]
    first_partners += [dev(0, 0, dy, dc) for dy in (1, 3, 2) for dc in range(NC)]
    first_partners += [dev(0, 0, 0, 1)]
    for partner in first_partners:
        pl.semaphore_signal(barrier, inc=1, device_id=partner, device_id_type=pl.DeviceIdType.MESH)
    count = len(first_partners)
    pl.semaphore_wait(barrier, count)

    def w_copy(s, flow, sub):
        if s == 8:
            src, dst = 11 + flow, 15
        else:
            src, dst = (0 if s == 1 else 2 * s - 3 + flow), 2 * s - 1 + flow
        rows = pl.ds(*PARTS[sub])
        source = wt_ref.at[rows] if s == 1 else wg.at[c, src, rows]
        return rcopy(source, wg.at[c, dst, rows], s_w.at[0], r_w.at[NP * (s - 1) + sub], dev(0, (1 - 2 * flow) * (2 if s == 8 else 1)))

    def w_start(s, flow, sub):
        w_copy(s, flow, sub).start()

    def w_sib(slot):
        k = min((slot + 1) // 2, 7)
        send(wg.at[c, slot], wg.at[c, slot], s_ws.at[0], r_ws.at[k], dev(0, 0, 0, 1))

    def first(sub):
        for flow in range(2):
            w_start(1, flow, sub)

    first(0)
    loads[1].wait()
    for half in range(2):
        ctxs[half] = ctx_v[half * SEQ:(half + 1) * SEQ, :].T
    lead = 1 - 2 * c
    ctx_sends_to = lambda dx, k: [
        send(ctxs.at[half], ctxg.at[x, c], s_ctx.at[0], r_ctx.at[k], (mod4(x + dx), z, y, half))
        for half in range(2)
    ]
    ctx_sends_to(lead, jnp.where(c == 0, 1, 4))
    send(ctxs.at[other], ctxg.at[x, c], s_ctx.at[1], r_ctx.at[0], dev(0, 0, 0, 1))
    loads[0].wait()
    w_sib(0)
    loads[2].wait()
    loads[3].wait()
    send(adg.at[c], adg.at[c], s_ad.at[0], r_ad.at[0], dev(0, 0, 0, 1))
    ctxg[x, c] = ctxs[c]

    loads[4].wait()
    loads[8].wait()
    lane = lax.broadcasted_iota(jnp.int32, (16, SEQ), 1)
    off = jnp.logical_not(diag)
    for half in range(2):
        rt[half, 0:HALF] = resid_v[half * SEQ:(half + 1) * SEQ, :].T
        rt[half, HALF:] = jnp.where(lane < len_v[half], 1.0, 0.0).astype(BF)

        @pl.when(jnp.logical_and(diag, c == half))
        def _():
            rrecv[c] = rt[half]

    send_unless(diag, rt.at[0], relay.at[y, c], s_res.at[0], r_res.at[0], (x, z, x, 0))
    send_unless(jnp.logical_or(off, c == 0), rt.at[0], rrecv.at[c], s_res.at[0], r_rel.at[c], (x, z, x, 0))
    first(1)
    first(2)
    for i in (5, 6, 7):
        loads[i].wait()

    @pl.when(diag)
    def _():
        buT[c] = bu_v[...].T
        gr[c] = jnp.concatenate([g_v[...], jnp.zeros((3, SEQ), F32)], axis=0)

    for dy in range(1, NY):
        send_unless(off, buT.at[c], buT.at[c], s_bu.at[0], r_bu.at[0], dev(0, 0, dy))
        send_unless(off, gr.at[c], gr.at[c], s_bu.at[1], r_bu.at[1], dev(0, 0, dy))

    first(3)
    first(4)
    def block(j):
        return mod4(x + j)

    def mm(js, k):
        lo, hi = CHUNKS[k]
        rows = (hi - lo) * COLS
        rhs = [jnp.concatenate([ctxg[block(j), cc] for j in js], axis=1) for cc in range(2)]
        lhs = [wg[cc, lo:hi].reshape(rows, HALF) for cc in range(2)]
        out = (dot(lhs[0], rhs[0]) + dot(lhs[1], rhs[1])).astype(BF)
        piece = pl.ds(lo * COLS, rows)
        for i, j in enumerate(js):
            part[j, piece] = out[:, i * SEQ:(i + 1) * SEQ]
            dest = mod4(x + j)
            send_unless(
                dest == y, part.at[j, piece], rsb.at[y, piece], s_rs.at[0], r_rs.at[k // (NCH - 1)], (x, z, dest, c)
            )

    def last_hop(flow):
        return (0, 2, 4) if flow == 0 else (1, 3)

    def w_take(s, sub):
        rows = pl.ds(*PARTS[sub])
        arrived(wg.at[0, 0, rows] if s == 8 else wg.at[pl.ds(0, 2), 0, rows], r_w.at[NP * (s - 1) + sub])
        for flow in range(2):
            if s < 7:
                w_start(s + 1, flow, sub)
            if s == 6 and sub in last_hop(flow):
                w_start(8, flow, sub)
        if sub == NP - 1:
            for slot in range(2 * s - 1, min(2 * s + 1, NZ)):
                w_sib(slot)

    def sib_wait(k):
        lo, hi = CHUNKS[k]
        arrived(wg.at[c, pl.ds(lo, hi - lo)], r_ws.at[k])

    def ctx_forward(i, dx_src, half_c, to_dx):
        blk = ctxg.at[mod4(x + dx_src), half_c]
        send(blk, blk, s_ctx.at[0], r_ctx.at[i], dev(to_dx))

    def ctx_wait(i):
        arrived(ctxg.at[0, 0], r_ctx.at[i])

    def low_rank_sum():
        acc = zp[pl.ds(pl.multiple_of(y * 32, 32), 32)]
        arrived(last_three(zr), r_zr.at[0])
        for dy in range(1, NY):
            acc = acc + zr[dy]
        zsum[...] = acc
        for dq in range(NX):
            me = jnp.logical_and(diag, dq == 0)
            send_unless(me, zsum, zall.at[y], s_zd.at[0], r_zd.at[0], (mod4(x + dq), z, x, c))

        @pl.when(diag)
        def _():
            zall[y] = acc

    def resid_half():
        send_unless(jnp.logical_and(diag, c == 1), rt.at[1], rrecv.at[c], s_res.at[1], r_rel.at[c], (y, z, x, 1))

    def second_leg():
        pass_on = jnp.logical_and(diag, c == 0)

        @pl.when(pass_on)
        def _():
            arrived(first_three(relay), r_res.at[0])

        for dq in range(1, NX):
            q = mod4(x + dq)
            for cc in range(2):
                send_unless(
                    jnp.logical_not(pass_on), relay.at[q, cc], rrecv.at[cc], s_rel.at[0], r_rel.at[cc], (q, z, x, 0)
                )

    def adapter_on():
        @pl.when(off)
        def _():
            arrived(buT.at[c], r_bu.at[0])
            arrived(gr.at[c], r_bu.at[1])

        send(buT.at[c], buT.at[c], s_bu.at[2], r_bu.at[2], dev(0, 0, 0, 1))
        send(gr.at[c], gr.at[c], s_bu.at[3], r_bu.at[3], dev(0, 0, 0, 1))

    def hop(s, *work):
        for sub in range(NP):
            w_take(s, sub)
            for f in work[len(work) * sub // NP:len(work) * (sub + 1) // NP]:
                f()

    def zp_sum():
        ctx_wait(0)
        arrived(adg.at[c], r_ad.at[0])
        zp[...] = dot(adg[0], ctxg[x, 0]) + dot(adg[1], ctxg[x, 1])

    def zp_send():
        for dy in range(1, NY):
            rows = pl.ds(pl.multiple_of(mod4(y + dy) * 32, 32), 32)
            send(zp.at[rows], zr.at[dy], s_zr.at[0], r_zr.at[0], dev(0, 0, dy))

    def ctx_near():
        ctx_wait(2)
        ctx_wait(3)

    def ctx_pass():
        ctx_wait(1)
        ctx_forward(5, -1, 0, 1)
        ctx_wait(4)
        ctx_forward(6, 1, 1, -1)

    def ctx_far():
        ctx_wait(5)
        ctx_wait(6)

    def m(js, *ks):
        return lambda: [mm(js, k) for k in ks]

    def sw(k):
        return lambda: sib_wait(k)

    ctx_second = lambda: ctx_sends_to(-lead, jnp.where(c == 0, 3, 2))

    def low_rank_terms():
        @pl.when(diag)
        def _():
            arrived(first_three(zall), r_zd.at[0])

        @pl.when(off)
        def _():
            arrived(zall, r_zd.at[0])

        arrived(buT.at[c], r_bu.at[2])
        arrived(gr.at[c], r_bu.at[3])
        zt = jnp.concatenate([zall[0], zall[1]], axis=0)
        ztt = jnp.concatenate([zall[2], zall[3]], axis=0)
        zero = jnp.zeros((RANK, SEQ), F32)
        rhs = jnp.concatenate([jnp.concatenate([ztt, zt], axis=0), jnp.concatenate([zt, zero], axis=0)], axis=1)
        r1, r2, r3 = split3(rhs)
        for cc in range(2):
            b = buT[cc]
            both = dot(b, r1) + dot(b, r2) + dot(b, r3)
            dh_ref[cc * HALF:(cc + 1) * HALF] = both[:, 0:SEQ]
            h_ref[cc * HALF:(cc + 1) * HALF] = both[:, SEQ:]

    def fold(v):
        return jnp.sum(v.reshape(-1, 8, SEQ), axis=0)

    def early_sums():
        for i in range(10):
            col = jnp.broadcast_to(gr[i // 5, pl.ds(i % 5, 1)], (SEQ, SEQ)).T
            gh_ref[i * SEQ:(i + 1) * SEQ] = col * col
        acc = jnp.zeros((SEQ, 3 * SEQ), F32)
        sums = [jnp.zeros((8, SEQ), F32) for _ in range(3)]
        lane = lax.broadcasted_iota(jnp.int32, (HALF, SEQ), 1)
        for cc in range(2):
            rows = pl.ds(cc * HALF, HALF)
            g2 = gh_ref[rows]
            d = dh_ref[rows]
            gd = g2 * d
            d1, d2 = split2(gd)
            k1, k2 = split2(jnp.where(lane < RANK, 1.0, g2))
            acc = acc + dot(buT[cc], jnp.concatenate([d1, d2, k1], axis=1), TN)
            e2 = dot(buT[cc], k2, TN)
            acc = acc + jnp.concatenate([jnp.zeros((SEQ, 2 * SEQ), F32), e2], axis=1)
            sums = [s + fold(t) for s, t in zip(sums, (d, gd, g2))]
        es[0, 0:RANK] = acc[0:RANK, 0:SEQ] + acc[0:RANK, SEQ:2 * SEQ]
        es[0, RANK:2 * RANK] = acc[0:RANK, 2 * SEQ:]
        for n, s in enumerate(sums):
            es[0, 2 * RANK + n:2 * RANK + n + 1] = jnp.sum(s, axis=0, keepdims=True)
        es[0, 2 * RANK + 3:] = jnp.zeros((5, SEQ), F32)

    def early_send():
        for dx in range(1, NX):
            send(es.at[0], es.at[dx], s_es.at[0], r_es.at[0], (mod4(x + dx), z, y, c))

    both = lambda *fs: lambda: [f() for f in fs]
    idle = lambda: None

    hop(1, ctx_second, zp_sum, zp_send)
    hop(2, sw(0), m((0,), 0), both(ctx_pass, low_rank_sum, resid_half))
    hop(3, both(sw(1), m((0,), 1)), idle, ctx_near)
    hop(4, both(sw(2), m((0,), 2), m((1, 3), 0)), both(m((1, 3), 1, 2)), adapter_on)
    hop(5, both(sw(3), m((0,), 3)), both(m((1, 3), 3), ctx_far), m((2,), 0, 1))
    hop(6, both(sw(4), m((1, 3), 4)), both(m((0, 2), 4), second_leg), m((2,), 2, 3))
    hop(7, both(sw(5), m((1, 3), 5)), m((0, 2), 5), low_rank_terms)
    hop(8, sw(6), m((1, 3), 6), m((0, 2), 6))
    sib_wait(7)
    mm((0, 1, 2, 3), 7)
    early_sums()
    early_send()

    for cc in range(2):
        @pl.when(jnp.logical_not(jnp.logical_and(diag, c == cc)))
        def _():
            arrived(rrecv.at[cc], r_rel.at[cc])
        h_ref[cc * HALF:(cc + 1) * HALF] = h_ref[cc * HALF:(cc + 1) * HALF] + rrecv[cc, 0:HALF].astype(F32)
    live = rrecv[0, HALF:].astype(F32)[0:1] * (1.0 / jnp.sqrt(jnp.float32(TOKENS)))

    jown = mod4(y - x)
    for k, (lo, hi) in enumerate(CHUNKS):
        if k in (0, NCH - 1):
            start = lo * COLS
            rows = pl.ds(start, (CHUNKS[-2][1] if k == 0 else hi) * COLS - start)
            arrived(rsb.at[pl.ds(0, 3), rows], r_rs.at[k // (NCH - 1)])
        for slot in range(lo, hi):
            step = (slot + 1) // 2
            zz = z if slot == 0 else (z - step if slot % 2 == 1 else z + step)
            zz = lax.rem(zz + NZ, NZ)
            rows = pl.ds(pl.multiple_of(zz * COLS, 16), COLS)
            piece = pl.ds(slot * COLS, COLS)
            acc = part[jown, piece].astype(F32)
            for dy in range(1, NY):
                acc = acc + rsb[mod4(y - dy), piece].astype(F32)
            h_ref[rows] = h_ref[rows] + acc

    acc = jnp.zeros((SEQ, 4 * SEQ), F32)
    sums = [jnp.zeros((8, SEQ), F32) for _ in range(6)]
    for cc in range(2):
        rows = pl.ds(cc * HALF, HALF)
        h = h_ref[rows]
        d = dh_ref[rows]
        g2 = gh_ref[rows]
        gh = g2 * h
        h1, h2 = split2(h)
        g1, g3 = split2(gh)
        acc = acc + dot(buT[cc], jnp.concatenate([h1, h2, g1, g3], axis=1), TN)
        sums = [s + fold(t) for s, t in zip(sums, (h, h * h, h * d, gh, gh * h, gh * d))]
    for n, s in enumerate(sums):
        ts[0, n:n + 1] = jnp.sum(s, axis=0, keepdims=True)
    ts[0, 6:] = jnp.zeros((2, SEQ), F32)
    for dx in (2, 1, 3):
        send(ts.at[0], ts.at[dx], s_ts.at[0], r_ts.at[0], (mod4(x + dx), z, y, c))
    ls[0, 0:RANK] = acc[0:RANK, 0:SEQ] + acc[0:RANK, SEQ:2 * SEQ]
    ls[0, RANK:] = acc[0:RANK, 2 * SEQ:3 * SEQ] + acc[0:RANK, 3 * SEQ:]
    for dx in (2, 1, 3):
        send(ls.at[0], ls.at[dx], s_st.at[0], r_st.at[0], (mod4(x + dx), z, y, c))
    early = es[0]
    arrived(last_three(es), r_es.at[0])
    for dx in range(1, NX):
        early = early + es[dx]
    late = ts[0]
    arrived(last_three(ts), r_ts.at[0])
    for dx in range(1, NX):
        late = late + ts[dx]
    inv = 1.0 / WIDTH
    m1, e_gd, e_g = [early[2 * RANK + n:2 * RANK + n + 1] * inv for n in range(3)]
    mu, e_hh, e_hd, e_gh, e_ghh, e_ghd = [late[n:n + 1] * inv for n in range(6)]
    rinv = lax.rsqrt(e_hh - mu * mu + 1e-05)
    m2 = rinv * (e_hd - mu * m1)
    g_n = rinv * (e_gh - mu * e_g)
    g_nn = rinv * rinv * (e_ghh - 2.0 * mu * e_gh + mu * mu * e_g)
    g_nd = rinv * (e_ghd - mu * e_gd)
    lr = live * rinv
    m3 = lr * (e_gd - m1 * e_g - m2 * g_n)
    m4 = lr * (g_nd - m1 * g_n - m2 * g_nn)
    late = ls[0]
    arrived(last_three(ls), r_st.at[0])
    for dx in range(1, NX):
        late = late + ls[dx]
    b_one = jnp.broadcast_to(early[RANK:2 * RANK, 0:1], (RANK, SEQ))
    b_g = jnp.broadcast_to(early[RANK:2 * RANK, SEQ - 1:SEQ], (RANK, SEQ))
    b_n = rinv * (late[0:RANK] - mu * b_one)
    b_gn = rinv * (late[RANK:2 * RANK] - mu * b_g)
    b_c = lr * (early[0:RANK] - m1 * b_g - m2 * b_gn)
    q1, q2 = split2(rinv * (b_c - m3 * b_one - m4 * b_n))
    xq = y
    qg[xq] = jnp.concatenate([q1, q2], axis=0).T
    for dy in (2, 1, 3):
        send(qg.at[xq], qg.at[xq], s_q.at[0], r_q.at[0], dev(0, 0, dy))

    z1, z2 = split2(jnp.concatenate([zall[0], zall[1]], axis=0))
    zs = jnp.concatenate([z1, z2], axis=0)
    for cc in range(2):
        rows = pl.ds(cc * HALF, HALF)
        n = (h_ref[rows] - mu) * rinv
        cot = lr * gh_ref[rows] * (dh_ref[rows] - m1 - n * m2)
        g1, g2 = split2(rinv * (cot - m3 - n * m4))
        hb = dot(zs, g1, NT) + dot(zs, g2, NT)
        hb = hb[0:RANK] + hb[RANK:]
        for p in range(NX):
            hb_snd[cc, p] = hb[16 * p:16 * (p + 1)]
    send(hb_snd.at[other], hb_sib, s_hs.at[0], r_hs.at[0], dev(0, 0, 0, 1))
    arrived(hb_sib, r_hs.at[0])
    hb_red[...] = hb_snd[c] + hb_sib[...]
    for dp in range(NX):
        p = mod4(x + dp)
        me = jnp.logical_and(diag, dp == 0)
        send_unless(me, hb_red.at[p], hb_rcv.at[y], s_hb.at[0], r_hb.at[0], (p, z, x, c))

    @pl.when(diag)
    def _():
        hb_rcv[y] = hb_red[x]

    arrived(first_three(qg), r_q.at[0])
    qs = jnp.concatenate([qg[xb] for xb in range(NX)], axis=0)
    mine = pl.ds(pl.multiple_of(x * 160, 32), 160)
    for cc in range(2):
        t = dot(jnp.concatenate([ctxg[xb, cc, mine] for xb in range(NX)], axis=1), qs)
        ha_snd[cc] = t + pltpu.roll(t, RANK, 1)
    send(ha_snd.at[other], ha_sib, s_ha.at[0], r_ha.at[0], dev(0, 0, 0, 1))
    arrived(ha_sib, r_ha.at[0])
    ha_sum[...] = ha_snd[c] + ha_sib[...]
    low = lax.broadcasted_iota(jnp.int32, (NZ, SEQ), 1) < RANK
    pairs = []
    for k in range(5):
        pairs.append(jnp.where(low, ha_sum[pl.ds(2 * k, NZ, stride=10)], ha_sum[pl.ds(2 * k + 1, NZ, stride=10)]))
    v = jnp.concatenate(pairs, axis=1)
    @pl.when(diag)
    def _():
        arrived(first_three(hb_rcv), r_hb.at[0])

    @pl.when(off)
    def _():
        arrived(hb_rcv, r_hb.at[0])

    v = jnp.concatenate([v, hb_rcv[0] + hb_rcv[1] + hb_rcv[2] + hb_rcv[3]], axis=1)
    for zi in range(NZ):
        ab[zi] = v[zi:zi + 1]
    for dz in (8, 7, 9, 6, 10, 5, 11, 4, 12, 3, 13, 2, 14, 1, 15):
        send(ab.at[lax.rem(z + dz, NZ)], abz.at[dz], s_ab.at[0], r_ab.at[0], dev(0, dz))
    acc = ab[z]
    arrived(abz.at[pl.ds(1, NZ - 1)], r_ab.at[0])
    for dz in range(1, NZ):
        acc = acc + abz[dz]
    for k in range(10):
        out_a[k:k + 1] = acc[:, k * RANK:(k + 1) * RANK]
    out_b[...] = acc[:, HALF:]

    left(wg.at[c, pl.ds(0, NZ - 1)], s_w.at[0])
    left(wg.at[c], s_ws.at[0])
    left(first_three(ctxg), s_ctx.at[0])
    left(ctxg.at[0, 0], s_ctx.at[1])
    left(adg.at[c], s_ad.at[0])
    for half in range(2):
        @pl.when(jnp.logical_not(jnp.logical_and(diag, c == half)))
        def _():
            left(rt.at[half], s_res.at[half])

    @pl.when(jnp.logical_and(diag, c == 0))
    def _():
        left(first_three(relay), s_rel.at[0])

    left(buT.at[c], s_bu.at[2])
    left(gr.at[c], s_bu.at[3])
    left(first_three(part), s_rs.at[0])
    left(first_three(zr), s_zr.at[0])
    left(first_three(es), s_es.at[0])
    left(first_three(ts), s_ts.at[0])
    left(first_three(ls), s_st.at[0])
    left(first_three(qg), s_q.at[0])
    left(hb_sib, s_hs.at[0])
    left(ha_sib, s_ha.at[0])
    left(ab.at[pl.ds(0, NZ - 1)], s_ab.at[0])

    @pl.when(diag)
    def _():
        left(ctxg.at[pl.ds(0, 3), 0], s_bu.at[0])
        left(first_three(ts), s_bu.at[1])
        left(first_three(zall), s_zd.at[0])
        left(first_three(hb_red), s_hb.at[0])

    @pl.when(off)
    def _():
        left(zall, s_zd.at[0])
        left(hb_red, s_hb.at[0])


def body(ctx, resid, w, a, b, d, u, gain, lengths):
    vmem = pl.BlockSpec(memory_space=pltpu.VMEM)
    dma = lambda *n: pltpu.SemaphoreType.DMA(n)
    return pl.pallas_call(
        kernel,
        out_shape=(jax.ShapeDtypeStruct((10, RANK), F32), jax.ShapeDtypeStruct((1, HALF), F32)),
        in_specs=[pl.BlockSpec(memory_space=pltpu.HBM)] * 9,
        out_specs=(vmem, vmem),
        scratch_shapes=[
            pltpu.VMEM((2 * SEQ, HALF), BF),
            pltpu.VMEM((2 * SEQ, HALF), BF),
            pltpu.VMEM((2 * RANK, HALF), BF),
            pltpu.VMEM((5, SEQ), F32),
            pltpu.SMEM((2,), jnp.int32),
            pltpu.VMEM((2, HALF, SEQ), BF),
            pltpu.VMEM((NX, NC, HALF, SEQ), BF),
            pltpu.VMEM((NC, NZ, COLS, HALF), BF),
            pltpu.VMEM((NC, 2 * RANK, HALF), BF),
            pltpu.VMEM((2, HALF + 16, SEQ), BF),
            pltpu.VMEM((NX, 2, HALF + 16, SEQ), BF),
            pltpu.VMEM((2, HALF + 16, SEQ), BF),
            pltpu.VMEM((NC, HALF, SEQ), BF),
            pltpu.VMEM((NC, 8, SEQ), F32),
            pltpu.VMEM((NX, FEATS, SEQ), BF),
            pltpu.VMEM((NY, FEATS, SEQ), BF),
            pltpu.VMEM((SEQ, SEQ), F32),
            pltpu.VMEM((NY, 32, SEQ), F32),
            pltpu.VMEM((32, SEQ), F32),
            pltpu.VMEM((NY, 32, SEQ), F32),
            pltpu.VMEM((NX, 2 * RANK + 8, SEQ), F32),
            pltpu.VMEM((NX, 8, SEQ), F32),
            pltpu.VMEM((NX, 2 * RANK, SEQ), F32),
            pltpu.VMEM((FEATS, SEQ), F32),
            pltpu.VMEM((FEATS, SEQ), F32),
            pltpu.VMEM((FEATS, SEQ), F32),
            pltpu.VMEM((NX, SEQ, SEQ), BF),
            pltpu.VMEM((NC, 160, SEQ), F32),
            pltpu.VMEM((160, SEQ), F32),
            pltpu.VMEM((NC, NX, 16, HALF), F32),
            pltpu.VMEM((NX, 16, HALF), F32),
            pltpu.VMEM((NX, 16, HALF), F32),
            pltpu.VMEM((NY, 16, HALF), F32),
            pltpu.VMEM((160, SEQ), F32),
            pltpu.VMEM((NZ, 1, 2 * HALF), F32),
            pltpu.VMEM((NZ, 1, 2 * HALF), F32),
            dma(9), dma(2), dma(7), dma(1), dma(8 * NP), dma(1), dma(NCH), dma(1), dma(1), dma(2), dma(1), dma(1), dma(2),
            dma(4), dma(4), dma(1), dma(2),
            dma(1), dma(1), dma(1), dma(1), dma(1), dma(1), dma(1), dma(1), dma(1), dma(1), dma(1), dma(1),
            dma(1), dma(1), dma(1), dma(1), dma(1), dma(1), dma(1), dma(1),
        ],
        compiler_params=pltpu.CompilerParams(collective_id=0, has_side_effects=True, vmem_limit_bytes=60 << 20),
        cost_estimate=pl.CostEstimate(flops=2 * 1280 * 1280 * 512, bytes_accessed=2 << 20, transcendentals=0),
        name="hvp",
    )(ctx, resid, w.T, a.T, d.T, b, u, gain.reshape(5, SEQ), lengths)


def solution(mesh):
    grid = Mesh(mesh.devices.reshape(NX, NZ, NY, NC), AXES)
    dp, tensor = ("x", "z"), ("y", "c")
    in_specs = (
        P(dp, tensor),
        P(dp, tensor),
        P(tensor, dp),
        P(tensor, None),
        P(None, tensor),
        P(tensor, None),
        P(None, tensor),
        P(tensor),
        P(dp),
    )
    out_specs = (P(("y", "c", "x", "z"), None), P(dp, tensor))
    return jax.shard_map(body, mesh=grid, in_specs=in_specs, out_specs=out_specs, check_vma=False)
```

```python
import functools

import jax
import jax.numpy as jnp
from jax import lax
from jax.experimental import pallas as pl
from jax.experimental.pallas import tpu as pltpu
from jax.sharding import Mesh, PartitionSpec as P

AXES = ("x", "z", "y", "c")
NX, NZ, NY, NC = 4, 16, 4, 2
SEQ = 128
RANK = 64
FEATS = 1280
HALF = 640
COLS = 80
TOKENS = 16384
WIDTH = 5120
BF = jnp.bfloat16
F32 = jnp.float32
CHUNKS = ((0, 1),) + tuple((2 * s - 1, 2 * s + 1) for s in range(1, 7)) + ((13, 16),)
PARTS = tuple((16 * i, 16) for i in range(5))
NP = len(PARTS)
NCH = len(CHUNKS)
NT = (((1,), (1,)), ((), ()))
TN = (((0,), (0,)), ((), ()))


def split2(v):
    hi = v.astype(BF)
    lo = (v - hi.astype(F32)).astype(BF)
    return hi, lo


def split3(v):
    hi = v.astype(BF)
    rest = v - hi.astype(F32)
    mid = rest.astype(BF)
    lo = (rest - mid.astype(F32)).astype(BF)
    return hi, mid, lo


def dot(a, b, dims=(((1,), (0,)), ((), ()))):
    return lax.dot_general(a, b, dims, preferred_element_type=F32)


def kernel(
    ctx_ref, resid_ref, wt_ref, at_ref, dt_ref, b_ref, u_ref, g_ref, len_ref,
    out_a, out_b,
    ctx_v, resid_v, bu_v, g_v, len_v,
    ctxs, ctxg, wg, adg, rt, relay, rrecv, buT, gr, part, rsb, zp, zr, zsum, zall, es, ts, ls, h_ref, dh_ref, gh_ref,
    qg, ha_snd, ha_sib, hb_snd, hb_sib, hb_red, hb_rcv, ha_sum, ab, abz,
    s_in, s_ctx, r_ctx, s_w, r_w, s_ws, r_ws, s_ad, r_ad, s_res, r_res, s_rel, r_rel, s_bu, r_bu, s_rs, r_rs,
    s_zr, r_zr, s_zd, r_zd, s_es, r_es, s_ts, r_ts, s_st, r_st, s_q, r_q, s_ha, r_ha, s_hs, r_hs, s_hb, r_hb, s_ab, r_ab,
):
    x, z, y, c = [lax.axis_index(a) for a in AXES]
    other = lax.rem(c + 1, NC)
    diag = x == y

    def mod4(v):
        return lax.rem(v + 8, 4)

    def dev(dx=0, dz=0, dy=0, dc=0):
        return (mod4(x + dx), lax.rem(z + dz + NZ, NZ), mod4(y + dy), lax.rem(c + dc, NC))

    def rcopy(src, dst, ss, rs, to):
        return pltpu.make_async_remote_copy(
            src_ref=src, dst_ref=dst, send_sem=ss, recv_sem=rs, device_id=to, device_id_type=pl.DeviceIdType.MESH
        )

    def arrived(dst, rs):
        rcopy(dst, dst, s_ad.at[0], rs, dev(0, 0, 0, 1)).wait_recv()

    def left(src, ss):
        rcopy(src, src, ss, r_ad.at[0], dev(0, 0, 0, 1)).wait_send()

    def send(src, dst, ss, rs, to):
        rcopy(src, dst, ss, rs, to).start()

    def send_unless(cond, src, dst, ss, rs, to):
        @pl.when(jnp.logical_not(cond))
        def _():
            send(src, dst, ss, rs, to)

    def first_three(ref):
        return ref.at[pl.ds(0, 3)]

    def last_three(ref):
        return ref.at[pl.ds(1, 3)]

    loads = [
        pltpu.make_async_copy(src, dst, s_in.at[i])
        for i, (src, dst) in enumerate((
            (wt_ref, wg.at[c, 0]),
            (ctx_ref, ctx_v),
            (at_ref, adg.at[c, pl.ds(0, RANK)]),
            (dt_ref, adg.at[c, pl.ds(RANK, RANK)]),
            (resid_ref, resid_v),
            (b_ref, bu_v.at[pl.ds(0, RANK)]),
            (u_ref, bu_v.at[pl.ds(RANK, RANK)]),
            (g_ref, g_v),
            (len_ref, len_v),
        ))
    ]
    for cp in loads:
        cp.start()

    barrier = pltpu.get_barrier_semaphore()
    first_partners = [dev(0, dz) for dz in (-1, 1)]
    first_partners += [dev(dx, 0, 0, dc) for dx in (1, 3, 2) for dc in range(NC)]
    first_partners += [dev(0, 0, dy, dc) for dy in (1, 3, 2) for dc in range(NC)]
    first_partners += [dev(0, 0, 0, 1)]
    for partner in first_partners:
        pl.semaphore_signal(barrier, inc=1, device_id=partner, device_id_type=pl.DeviceIdType.MESH)
    count = len(first_partners)
    pl.semaphore_wait(barrier, count)

    def w_copy(s, flow, sub):
        if s == 8:
            src, dst = 11 + flow, 15
        else:
            src, dst = (0 if s == 1 else 2 * s - 3 + flow), 2 * s - 1 + flow
        rows = pl.ds(*PARTS[sub])
        source = wt_ref.at[rows] if s == 1 else wg.at[c, src, rows]
        return rcopy(source, wg.at[c, dst, rows], s_w.at[0], r_w.at[NP * (s - 1) + sub], dev(0, (1 - 2 * flow) * (2 if s == 8 else 1)))

    def w_start(s, flow, sub):
        w_copy(s, flow, sub).start()

    def w_sib(slot):
        k = min((slot + 1) // 2, 7)
        send(wg.at[c, slot], wg.at[c, slot], s_ws.at[0], r_ws.at[k], dev(0, 0, 0, 1))

    def first(sub):
        for flow in range(2):
            w_start(1, flow, sub)

    first(0)
    loads[1].wait()
    for half in range(2):
        ctxs[half] = ctx_v[half * SEQ:(half + 1) * SEQ, :].T
    lead = 1 - 2 * c
    ctx_sends_to = lambda dx, k: [
        send(ctxs.at[half], ctxg.at[x, c], s_ctx.at[0], r_ctx.at[k], (mod4(x + dx), z, y, half))
        for half in range(2)
    ]
    ctx_sends_to(lead, jnp.where(c == 0, 1, 4))
    send(ctxs.at[other], ctxg.at[x, c], s_ctx.at[1], r_ctx.at[0], dev(0, 0, 0, 1))
    loads[0].wait()
    w_sib(0)
    loads[2].wait()
    loads[3].wait()
    send(adg.at[c], adg.at[c], s_ad.at[0], r_ad.at[0], dev(0, 0, 0, 1))
    ctxg[x, c] = ctxs[c]

    loads[4].wait()
    loads[8].wait()
    lane = lax.broadcasted_iota(jnp.int32, (16, SEQ), 1)
    off = jnp.logical_not(diag)
    for half in range(2):
        rt[half, 0:HALF] = resid_v[half * SEQ:(half + 1) * SEQ, :].T
        rt[half, HALF:] = jnp.where(lane < len_v[half], 1.0, 0.0).astype(BF)

        @pl.when(jnp.logical_and(diag, c == half))
        def _():
            rrecv[c] = rt[half]

    send_unless(diag, rt.at[0], relay.at[y, c], s_res.at[0], r_res.at[0], (x, z, x, 0))
    send_unless(jnp.logical_or(off, c == 0), rt.at[0], rrecv.at[c], s_res.at[0], r_rel.at[c], (x, z, x, 0))
    first(1)
    first(2)
    for i in (5, 6, 7):
        loads[i].wait()

    @pl.when(diag)
    def _():
        buT[c] = bu_v[...].T
        gr[c] = jnp.concatenate([g_v[...], jnp.zeros((3, SEQ), F32)], axis=0)

    for dy in range(1, NY):
        send_unless(off, buT.at[c], buT.at[c], s_bu.at[0], r_bu.at[0], dev(0, 0, dy))
        send_unless(off, gr.at[c], gr.at[c], s_bu.at[1], r_bu.at[1], dev(0, 0, dy))

    first(3)
    first(4)
    def block(j):
        return mod4(x + j)

    def mm(js, k):
        lo, hi = CHUNKS[k]
        rows = (hi - lo) * COLS
        rhs = [jnp.concatenate([ctxg[block(j), cc] for j in js], axis=1) for cc in range(2)]
        lhs = [wg[cc, lo:hi].reshape(rows, HALF) for cc in range(2)]
        out = (dot(lhs[0], rhs[0]) + dot(lhs[1], rhs[1])).astype(BF)
        piece = pl.ds(lo * COLS, rows)
        for i, j in enumerate(js):
            part[j, piece] = out[:, i * SEQ:(i + 1) * SEQ]
            dest = mod4(x + j)
            send_unless(
                dest == y, part.at[j, piece], rsb.at[y, piece], s_rs.at[0], r_rs.at[k // (NCH - 1)], (x, z, dest, c)
            )

    def last_hop(flow):
        return (0, 2, 4) if flow == 0 else (1, 3)

    def w_take(s, sub):
        rows = pl.ds(*PARTS[sub])
        arrived(wg.at[0, 0, rows] if s == 8 else wg.at[pl.ds(0, 2), 0, rows], r_w.at[NP * (s - 1) + sub])
        for flow in range(2):
            if s < 7:
                w_start(s + 1, flow, sub)
            if s == 6 and sub in last_hop(flow):
                w_start(8, flow, sub)
        if sub == NP - 1:
            for slot in range(2 * s - 1, min(2 * s + 1, NZ)):
                w_sib(slot)

    def sib_wait(k):
        lo, hi = CHUNKS[k]
        arrived(wg.at[c, pl.ds(lo, hi - lo)], r_ws.at[k])

    def ctx_forward(i, dx_src, half_c, to_dx):
        blk = ctxg.at[mod4(x + dx_src), half_c]
        send(blk, blk, s_ctx.at[0], r_ctx.at[i], dev(to_dx))

    def ctx_wait(i):
        arrived(ctxg.at[0, 0], r_ctx.at[i])

    def low_rank_sum():
        acc = zp[pl.ds(pl.multiple_of(y * 32, 32), 32)]
        arrived(last_three(zr), r_zr.at[0])
        for dy in range(1, NY):
            acc = acc + zr[dy]
        zsum[...] = acc
        for dq in range(NX):
            me = jnp.logical_and(diag, dq == 0)
            send_unless(me, zsum, zall.at[y], s_zd.at[0], r_zd.at[0], (mod4(x + dq), z, x, c))

        @pl.when(diag)
        def _():
            zall[y] = acc

    def resid_half():
        send_unless(jnp.logical_and(diag, c == 1), rt.at[1], rrecv.at[c], s_res.at[1], r_rel.at[c], (y, z, x, 1))

    def second_leg():
        pass_on = jnp.logical_and(diag, c == 0)

        @pl.when(pass_on)
        def _():
            arrived(first_three(relay), r_res.at[0])

        for dq in range(1, NX):
            q = mod4(x + dq)
            for cc in range(2):
                send_unless(
                    jnp.logical_not(pass_on), relay.at[q, cc], rrecv.at[cc], s_rel.at[0], r_rel.at[cc], (q, z, x, 0)
                )

    def adapter_on():
        @pl.when(off)
        def _():
            arrived(buT.at[c], r_bu.at[0])
            arrived(gr.at[c], r_bu.at[1])

        send(buT.at[c], buT.at[c], s_bu.at[2], r_bu.at[2], dev(0, 0, 0, 1))
        send(gr.at[c], gr.at[c], s_bu.at[3], r_bu.at[3], dev(0, 0, 0, 1))

    def hop(s, *work):
        for sub in range(NP):
            w_take(s, sub)
            for f in work[len(work) * sub // NP:len(work) * (sub + 1) // NP]:
                f()

    def zp_sum():
        ctx_wait(0)
        arrived(adg.at[c], r_ad.at[0])
        zp[...] = dot(adg[0], ctxg[x, 0]) + dot(adg[1], ctxg[x, 1])

    def zp_send():
        for dy in range(1, NY):
            rows = pl.ds(pl.multiple_of(mod4(y + dy) * 32, 32), 32)
            send(zp.at[rows], zr.at[dy], s_zr.at[0], r_zr.at[0], dev(0, 0, dy))

    def ctx_near():
        ctx_wait(2)
        ctx_wait(3)

    def ctx_pass():
        ctx_wait(1)
        ctx_forward(5, -1, 0, 1)
        ctx_wait(4)
        ctx_forward(6, 1, 1, -1)

    def ctx_far():
        ctx_wait(5)
        ctx_wait(6)

    def m(js, *ks):
        return lambda: [mm(js, k) for k in ks]

    def sw(k):
        return lambda: sib_wait(k)

    ctx_second = lambda: ctx_sends_to(-lead, jnp.where(c == 0, 3, 2))

    def low_rank_terms():
        @pl.when(diag)
        def _():
            arrived(first_three(zall), r_zd.at[0])

        @pl.when(off)
        def _():
            arrived(zall, r_zd.at[0])

        arrived(buT.at[c], r_bu.at[2])
        arrived(gr.at[c], r_bu.at[3])
        zt = jnp.concatenate([zall[0], zall[1]], axis=0)
        ztt = jnp.concatenate([zall[2], zall[3]], axis=0)
        zero = jnp.zeros((RANK, SEQ), F32)
        rhs = jnp.concatenate([jnp.concatenate([ztt, zt], axis=0), jnp.concatenate([zt, zero], axis=0)], axis=1)
        r1, r2, r3 = split3(rhs)
        for cc in range(2):
            b = buT[cc]
            both = dot(b, r1) + dot(b, r2) + dot(b, r3)
            dh_ref[cc * HALF:(cc + 1) * HALF] = both[:, 0:SEQ]
            h_ref[cc * HALF:(cc + 1) * HALF] = both[:, SEQ:]

    def fold(v):
        return jnp.sum(v.reshape(-1, 8, SEQ), axis=0)

    def early_sums():
        for i in range(10):
            col = jnp.broadcast_to(gr[i // 5, pl.ds(i % 5, 1)], (SEQ, SEQ)).T
            gh_ref[i * SEQ:(i + 1) * SEQ] = col * col
        acc = jnp.zeros((SEQ, 3 * SEQ), F32)
        sums = [jnp.zeros((8, SEQ), F32) for _ in range(3)]
        lane = lax.broadcasted_iota(jnp.int32, (HALF, SEQ), 1)
        for cc in range(2):
            rows = pl.ds(cc * HALF, HALF)
            g2 = gh_ref[rows]
            d = dh_ref[rows]
            gd = g2 * d
            d1, d2 = split2(gd)
            k1, k2 = split2(jnp.where(lane < RANK, 1.0, g2))
            acc = acc + dot(buT[cc], jnp.concatenate([d1, d2, k1], axis=1), TN)
            e2 = dot(buT[cc], k2, TN)
            acc = acc + jnp.concatenate([jnp.zeros((SEQ, 2 * SEQ), F32), e2], axis=1)
            sums = [s + fold(t) for s, t in zip(sums, (d, gd, g2))]
        es[0, 0:RANK] = acc[0:RANK, 0:SEQ] + acc[0:RANK, SEQ:2 * SEQ]
        es[0, RANK:2 * RANK] = acc[0:RANK, 2 * SEQ:]
        for n, s in enumerate(sums):
            es[0, 2 * RANK + n:2 * RANK + n + 1] = jnp.sum(s, axis=0, keepdims=True)
        es[0, 2 * RANK + 3:] = jnp.zeros((5, SEQ), F32)

    def early_send():
        for dx in range(1, NX):
            send(es.at[0], es.at[dx], s_es.at[0], r_es.at[0], (mod4(x + dx), z, y, c))

    both = lambda *fs: lambda: [f() for f in fs]
    idle = lambda: None

    hop(1, ctx_second, zp_sum, zp_send)
    hop(2, sw(0), m((0,), 0), both(ctx_pass, low_rank_sum, resid_half))
    hop(3, both(sw(1), m((0,), 1)), idle, ctx_near)
    hop(4, both(sw(2), m((0,), 2), m((1, 3), 0)), both(m((1, 3), 1, 2)), adapter_on)
    hop(5, both(sw(3), m((0,), 3)), both(m((1, 3), 3), ctx_far), m((2,), 0, 1))
    hop(6, both(sw(4), m((1, 3), 4)), both(m((0, 2), 4), second_leg), m((2,), 2, 3))
    hop(7, both(sw(5), m((1, 3), 5)), m((0, 2), 5), idle)
    hop(8)
    sib_wait(6)
    mm((0, 1, 2, 3), 6)
    sib_wait(7)
    mm((0, 1, 2, 3), 7)
    low_rank_terms()
    early_sums()
    early_send()

    for cc in range(2):
        @pl.when(jnp.logical_not(jnp.logical_and(diag, c == cc)))
        def _():
            arrived(rrecv.at[cc], r_rel.at[cc])
        h_ref[cc * HALF:(cc + 1) * HALF] = h_ref[cc * HALF:(cc + 1) * HALF] + rrecv[cc, 0:HALF].astype(F32)
    live = rrecv[0, HALF:].astype(F32)[0:1] * (1.0 / jnp.sqrt(jnp.float32(TOKENS)))

    jown = mod4(y - x)
    for k, (lo, hi) in enumerate(CHUNKS):
        if k in (0, NCH - 1):
            start = lo * COLS
            rows = pl.ds(start, (CHUNKS[-2][1] if k == 0 else hi) * COLS - start)
            arrived(rsb.at[pl.ds(0, 3), rows], r_rs.at[k // (NCH - 1)])
        for slot in range(lo, hi):
            step = (slot + 1) // 2
            zz = z if slot == 0 else (z - step if slot % 2 == 1 else z + step)
            zz = lax.rem(zz + NZ, NZ)
            rows = pl.ds(pl.multiple_of(zz * COLS, 16), COLS)
            piece = pl.ds(slot * COLS, COLS)
            acc = part[jown, piece].astype(F32)
            for dy in range(1, NY):
                acc = acc + rsb[mod4(y - dy), piece].astype(F32)
            h_ref[rows] = h_ref[rows] + acc

    acc = jnp.zeros((SEQ, 4 * SEQ), F32)
    sums = [jnp.zeros((8, SEQ), F32) for _ in range(6)]
    for cc in range(2):
        rows = pl.ds(cc * HALF, HALF)
        h = h_ref[rows]
        d = dh_ref[rows]
        g2 = gh_ref[rows]
        gh = g2 * h
        h1, h2 = split2(h)
        g1, g3 = split2(gh)
        acc = acc + dot(buT[cc], jnp.concatenate([h1, h2, g1, g3], axis=1), TN)
        sums = [s + fold(t) for s, t in zip(sums, (h, h * h, h * d, gh, gh * h, gh * d))]
    for n, s in enumerate(sums):
        ts[0, n:n + 1] = jnp.sum(s, axis=0, keepdims=True)
    ts[0, 6:] = jnp.zeros((2, SEQ), F32)
    for dx in (2, 1, 3):
        send(ts.at[0], ts.at[dx], s_ts.at[0], r_ts.at[0], (mod4(x + dx), z, y, c))
    ls[0, 0:RANK] = acc[0:RANK, 0:SEQ] + acc[0:RANK, SEQ:2 * SEQ]
    ls[0, RANK:] = acc[0:RANK, 2 * SEQ:3 * SEQ] + acc[0:RANK, 3 * SEQ:]
    for dx in (2, 1, 3):
        send(ls.at[0], ls.at[dx], s_st.at[0], r_st.at[0], (mod4(x + dx), z, y, c))
    early = es[0]
    arrived(last_three(es), r_es.at[0])
    for dx in range(1, NX):
        early = early + es[dx]
    late = ts[0]
    arrived(last_three(ts), r_ts.at[0])
    for dx in range(1, NX):
        late = late + ts[dx]
    inv = 1.0 / WIDTH
    m1, e_gd, e_g = [early[2 * RANK + n:2 * RANK + n + 1] * inv for n in range(3)]
    mu, e_hh, e_hd, e_gh, e_ghh, e_ghd = [late[n:n + 1] * inv for n in range(6)]
    rinv = lax.rsqrt(e_hh - mu * mu + 1e-05)
    m2 = rinv * (e_hd - mu * m1)
    g_n = rinv * (e_gh - mu * e_g)
    g_nn = rinv * rinv * (e_ghh - 2.0 * mu * e_gh + mu * mu * e_g)
    g_nd = rinv * (e_ghd - mu * e_gd)
    lr = live * rinv
    m3 = lr * (e_gd - m1 * e_g - m2 * g_n)
    m4 = lr * (g_nd - m1 * g_n - m2 * g_nn)
    late = ls[0]
    arrived(last_three(ls), r_st.at[0])
    for dx in range(1, NX):
        late = late + ls[dx]
    b_one = jnp.broadcast_to(early[RANK:2 * RANK, 0:1], (RANK, SEQ))
    b_g = jnp.broadcast_to(early[RANK:2 * RANK, SEQ - 1:SEQ], (RANK, SEQ))
    b_n = rinv * (late[0:RANK] - mu * b_one)
    b_gn = rinv * (late[RANK:2 * RANK] - mu * b_g)
    b_c = lr * (early[0:RANK] - m1 * b_g - m2 * b_gn)
    q1, q2 = split2(rinv * (b_c - m3 * b_one - m4 * b_n))
    xq = y
    qg[xq] = jnp.concatenate([q1, q2], axis=0).T
    for dy in (2, 1, 3):
        send(qg.at[xq], qg.at[xq], s_q.at[0], r_q.at[0], dev(0, 0, dy))

    z1, z2 = split2(jnp.concatenate([zall[0], zall[1]], axis=0))
    zs = jnp.concatenate([z1, z2], axis=0)
    for cc in range(2):
        rows = pl.ds(cc * HALF, HALF)
        n = (h_ref[rows] - mu) * rinv
        cot = lr * gh_ref[rows] * (dh_ref[rows] - m1 - n * m2)
        g1, g2 = split2(rinv * (cot - m3 - n * m4))
        hb = dot(zs, g1, NT) + dot(zs, g2, NT)
        hb = hb[0:RANK] + hb[RANK:]
        for p in range(NX):
            hb_snd[cc, p] = hb[16 * p:16 * (p + 1)]
    send(hb_snd.at[other], hb_sib, s_hs.at[0], r_hs.at[0], dev(0, 0, 0, 1))
    arrived(hb_sib, r_hs.at[0])
    hb_red[...] = hb_snd[c] + hb_sib[...]
    for dp in range(NX):
        p = mod4(x + dp)
        me = jnp.logical_and(diag, dp == 0)
        send_unless(me, hb_red.at[p], hb_rcv.at[y], s_hb.at[0], r_hb.at[0], (p, z, x, c))

    @pl.when(diag)
    def _():
        hb_rcv[y] = hb_red[x]

    arrived(first_three(qg), r_q.at[0])
    qs = jnp.concatenate([qg[xb] for xb in range(NX)], axis=0)
    mine = pl.ds(pl.multiple_of(x * 160, 32), 160)
    for cc in range(2):
        t = dot(jnp.concatenate([ctxg[xb, cc, mine] for xb in range(NX)], axis=1), qs)
        ha_snd[cc] = t + pltpu.roll(t, RANK, 1)
    send(ha_snd.at[other], ha_sib, s_ha.at[0], r_ha.at[0], dev(0, 0, 0, 1))
    arrived(ha_sib, r_ha.at[0])
    ha_sum[...] = ha_snd[c] + ha_sib[...]
    low = lax.broadcasted_iota(jnp.int32, (NZ, SEQ), 1) < RANK
    pairs = []
    for k in range(5):
        pairs.append(jnp.where(low, ha_sum[pl.ds(2 * k, NZ, stride=10)], ha_sum[pl.ds(2 * k + 1, NZ, stride=10)]))
    v = jnp.concatenate(pairs, axis=1)
    @pl.when(diag)
    def _():
        arrived(first_three(hb_rcv), r_hb.at[0])

    @pl.when(off)
    def _():
        arrived(hb_rcv, r_hb.at[0])

    v = jnp.concatenate([v, hb_rcv[0] + hb_rcv[1] + hb_rcv[2] + hb_rcv[3]], axis=1)
    for zi in range(NZ):
        ab[zi] = v[zi:zi + 1]
    for dz in (8, 7, 9, 6, 10, 5, 11, 4, 12, 3, 13, 2, 14, 1, 15):
        send(ab.at[lax.rem(z + dz, NZ)], abz.at[dz], s_ab.at[0], r_ab.at[0], dev(0, dz))
    acc = ab[z]
    arrived(abz.at[pl.ds(1, NZ - 1)], r_ab.at[0])
    for dz in range(1, NZ):
        acc = acc + abz[dz]
    for k in range(10):
        out_a[k:k + 1] = acc[:, k * RANK:(k + 1) * RANK]
    out_b[...] = acc[:, HALF:]

    left(wg.at[c, pl.ds(0, NZ - 1)], s_w.at[0])
    left(wg.at[c], s_ws.at[0])
    left(first_three(ctxg), s_ctx.at[0])
    left(ctxg.at[0, 0], s_ctx.at[1])
    left(adg.at[c], s_ad.at[0])
    for half in range(2):
        @pl.when(jnp.logical_not(jnp.logical_and(diag, c == half)))
        def _():
            left(rt.at[half], s_res.at[half])

    @pl.when(jnp.logical_and(diag, c == 0))
    def _():
        left(first_three(relay), s_rel.at[0])

    left(buT.at[c], s_bu.at[2])
    left(gr.at[c], s_bu.at[3])
    left(first_three(part), s_rs.at[0])
    left(first_three(zr), s_zr.at[0])
    left(first_three(es), s_es.at[0])
    left(first_three(ts), s_ts.at[0])
    left(first_three(ls), s_st.at[0])
    left(first_three(qg), s_q.at[0])
    left(hb_sib, s_hs.at[0])
    left(ha_sib, s_ha.at[0])
    left(ab.at[pl.ds(0, NZ - 1)], s_ab.at[0])

    @pl.when(diag)
    def _():
        left(ctxg.at[pl.ds(0, 3), 0], s_bu.at[0])
        left(first_three(ts), s_bu.at[1])
        left(first_three(zall), s_zd.at[0])
        left(first_three(hb_red), s_hb.at[0])

    @pl.when(off)
    def _():
        left(zall, s_zd.at[0])
        left(hb_red, s_hb.at[0])


def body(ctx, resid, w, a, b, d, u, gain, lengths):
    vmem = pl.BlockSpec(memory_space=pltpu.VMEM)
    dma = lambda *n: pltpu.SemaphoreType.DMA(n)
    return pl.pallas_call(
        kernel,
        out_shape=(jax.ShapeDtypeStruct((10, RANK), F32), jax.ShapeDtypeStruct((1, HALF), F32)),
        in_specs=[pl.BlockSpec(memory_space=pltpu.HBM)] * 9,
        out_specs=(vmem, vmem),
        scratch_shapes=[
            pltpu.VMEM((2 * SEQ, HALF), BF),
            pltpu.VMEM((2 * SEQ, HALF), BF),
            pltpu.VMEM((2 * RANK, HALF), BF),
            pltpu.VMEM((5, SEQ), F32),
            pltpu.SMEM((2,), jnp.int32),
            pltpu.VMEM((2, HALF, SEQ), BF),
            pltpu.VMEM((NX, NC, HALF, SEQ), BF),
            pltpu.VMEM((NC, NZ, COLS, HALF), BF),
            pltpu.VMEM((NC, 2 * RANK, HALF), BF),
            pltpu.VMEM((2, HALF + 16, SEQ), BF),
            pltpu.VMEM((NX, 2, HALF + 16, SEQ), BF),
            pltpu.VMEM((2, HALF + 16, SEQ), BF),
            pltpu.VMEM((NC, HALF, SEQ), BF),
            pltpu.VMEM((NC, 8, SEQ), F32),
            pltpu.VMEM((NX, FEATS, SEQ), BF),
            pltpu.VMEM((NY, FEATS, SEQ), BF),
            pltpu.VMEM((SEQ, SEQ), F32),
            pltpu.VMEM((NY, 32, SEQ), F32),
            pltpu.VMEM((32, SEQ), F32),
            pltpu.VMEM((NY, 32, SEQ), F32),
            pltpu.VMEM((NX, 2 * RANK + 8, SEQ), F32),
            pltpu.VMEM((NX, 8, SEQ), F32),
            pltpu.VMEM((NX, 2 * RANK, SEQ), F32),
            pltpu.VMEM((FEATS, SEQ), F32),
            pltpu.VMEM((FEATS, SEQ), F32),
            pltpu.VMEM((FEATS, SEQ), F32),
            pltpu.VMEM((NX, SEQ, SEQ), BF),
            pltpu.VMEM((NC, 160, SEQ), F32),
            pltpu.VMEM((160, SEQ), F32),
            pltpu.VMEM((NC, NX, 16, HALF), F32),
            pltpu.VMEM((NX, 16, HALF), F32),
            pltpu.VMEM((NX, 16, HALF), F32),
            pltpu.VMEM((NY, 16, HALF), F32),
            pltpu.VMEM((160, SEQ), F32),
            pltpu.VMEM((NZ, 1, 2 * HALF), F32),
            pltpu.VMEM((NZ, 1, 2 * HALF), F32),
            dma(9), dma(2), dma(7), dma(1), dma(8 * NP), dma(1), dma(NCH), dma(1), dma(1), dma(2), dma(1), dma(1), dma(2),
            dma(4), dma(4), dma(1), dma(2),
            dma(1), dma(1), dma(1), dma(1), dma(1), dma(1), dma(1), dma(1), dma(1), dma(1), dma(1), dma(1),
            dma(1), dma(1), dma(1), dma(1), dma(1), dma(1), dma(1), dma(1),
        ],
        compiler_params=pltpu.CompilerParams(collective_id=0, has_side_effects=True, vmem_limit_bytes=60 << 20),
        cost_estimate=pl.CostEstimate(flops=2 * 1280 * 1280 * 512, bytes_accessed=2 << 20, transcendentals=0),
        name="hvp",
    )(ctx, resid, w.T, a.T, d.T, b, u, gain.reshape(5, SEQ), lengths)


def solution(mesh):
    grid = Mesh(mesh.devices.reshape(NX, NZ, NY, NC), AXES)
    dp, tensor = ("x", "z"), ("y", "c")
    in_specs = (
        P(dp, tensor),
        P(dp, tensor),
        P(tensor, dp),
        P(tensor, None),
        P(None, tensor),
        P(tensor, None),
        P(None, tensor),
        P(tensor),
        P(dp),
    )
    out_specs = (P(("y", "c", "x", "z"), None), P(dp, tensor))
    return jax.shard_map(body, mesh=grid, in_specs=in_specs, out_specs=out_specs, check_vma=False)
```
